128 devices in a mesh: dp: 4 (over x), expert: 32 (over z, y, core).
Axes of the slice: x: 4, y: 4, z: 4, core: 2. Of those that a mesh axis runs over, the one named last changes fastest.
Arguments:
- tokens: bfloat16 [4096, 7168], P('expert', 'dp'), may hold values from -6 to 6
- cotangent: bfloat16 [4096, 7168], P('expert', 'dp'), may hold values from -6 to 6
- routes: int32 [4096, 4], P('expert'), may hold values from 0 to 31, all different within a row; in each aligned block of 128 rows (0 to 127, 128 to 255, ...) at most 24 rows name the same one
- gates: float32 [4096, 4], P('expert'), may hold values from 0.2 to 1
- w_gate: bfloat16 [32, 7168, 1024], P('expert', 'dp'), may hold values from -0.0625 to 0.0625
- w_up: bfloat16 [32, 7168, 1024], P('expert', 'dp'), may hold values from -0.0625 to 0.0625
- w_down: bfloat16 [32, 1024, 7168], P('expert', None, 'dp'), may hold values from -0.1875 to 0.1875
Outputs:
- mixed: bfloat16 [4096, 7168], P('expert', 'dp')
- input_grad: bfloat16 [4096, 7168], P('expert', 'dp')
- grad_w_gate: bfloat16 [32, 7168, 1024], P('expert', 'dp')
- grad_w_up: bfloat16 [32, 7168, 1024], P('expert', 'dp')
- grad_w_down: bfloat16 [32, 1024, 7168], P('expert', None, 'dp')
The draws below stay inside these ranges and needn't reach their ends.
Inputs may be any that keep to these rules, and one draw needn't show every extreme that they name: `routes`: A row names 4 different experts; in each aligned block of 128 rows (the tokens of one index of expert) no expert is named by more than 24 rows, a bound that some block reaches.
All inputs are finite; a program needn't handle non-finite values.
Results may differ from the reference program's by a relative error of at most 0.019.
Values may be sent and summed in bfloat16 or wider, within the bound.
A program may use at most 128 MiB of HBM per device.

```python
import math
import jax
import jax.numpy as jnp
import numpy as np
from jax import lax

D = 7168
H = 1024
TOP = 4
TOK_DEV = 128
EXPERTS = 32
TOKENS = 4096
CAP = 24
ROWS = 768
D_PART = 1792
N_DP = 4
N_EXPERT = 32


def steps_of(own_key, shape, pieces, smallest, top_value):
    def one(axis_at, parts):
        steps = jax.random.uniform(jax.random.fold_in(jax.random.fold_in(own_key, 6), axis_at), (parts,), jnp.float32, smallest / len(pieces), top_value / len(pieces))
        return jnp.repeat(jnp.exp(steps), shape[axis_at] // parts).reshape((-1,) + (1,) * (len(shape) - axis_at - 1))

    gain = one(*pieces[0])
    for cut in pieces[1:]:
        gain = gain * one(*cut)
    return gain


def assign_block(own_key, own, number, rows, count, top, limit, skew):
    sequence = jax.random.permutation(own_key, count)
    packed, usual = portions_of(count, rows * top, limit, skew, True), portions_of(count, rows * top, limit, skew, False)
    places = jnp.arange(count)

    def named(sizes, turn):
        used = int((sizes > 0).sum())
        fixed = max(1, used // 4)
        shifted = fixed + (places - fixed + turn * (used - fixed)) % max(1, count - fixed)
        return jnp.zeros((count,), jnp.int32).at[sequence[jnp.where(places < fixed, places, shifted)]].set(jnp.asarray(sizes, jnp.int32))

    sizes = jnp.where(number % 4 == 0, named(packed, number // 4), named(usual, number - number // 4 - 1))
    mixed = jax.random.permutation(jax.random.fold_in(own, 3), count)
    donor, sink = mixed[0:count // 2 * 2:2], mixed[1:count // 2 * 2:2]
    room = jnp.minimum(sizes[donor] - 1, limit - sizes[sink]) // 2
    room = jnp.where((donor == sequence[0]) | (sink == sequence[0]) | (sizes[sink] == 0), 0, jnp.maximum(room, 0))
    shifted = jax.random.randint(jax.random.fold_in(own, 4), (count // 2,), 0, 1 << 20) % (room + 1)
    sizes = sizes.at[donor].add(-shifted).at[sink].add(shifted)
    labels = jnp.searchsorted(jnp.cumsum(sizes), jnp.arange(rows * top), side="right").astype(jnp.int32)
    table = labels.reshape(top, rows).T
    table = table[jax.random.permutation(jax.random.fold_in(own, 1), rows)]
    turn = jax.random.randint(jax.random.fold_in(own, 2), (rows, 1), 0, top)
    return jnp.take_along_axis(table, (jnp.arange(top)[None, :] + turn) % top, axis=1)


def portions_of(number_of, total, most, lean, full):
    loads = [(1 << 20) // math.isqrt(rank ** lean) + 1 for rank in range(1, number_of + 1)]
    largest = most if full else min(most, max(-(-total // number_of), total * loads[0] // sum(loads)))
    least = 1 if total - largest >= number_of - 1 else 0
    given, surplus = [largest] + [least] * (number_of - 1), total - largest - least * (number_of - 1)
    while surplus > 0:
        candidates = [i for i in range(1, number_of) if given[i] < largest] or [i for i in range(1, number_of) if given[i] < most]
        mass, remaining = sum([loads[i] for i in candidates]), surplus
        for i in candidates:
            more = min(most - given[i], max(1, remaining * loads[i] // mass), surplus)
            given[i] = given[i] + more
            surplus = surplus - more
    return np.array(given)


def scatter_about(stream_key, dims, scale, bound, pieces=(), kind=jnp.bfloat16):
    result = jax.random.normal(stream_key, dims, jnp.float32) * scale
    if len(pieces) > 0:
        result = steps_of(stream_key, dims, pieces, -0.22, 0.18) * result
    return jnp.clip(result, min=-bound, max=bound).astype(kind)


def setup_inputs(seed: int = 0) -> dict:
    seeds = jax.random.split(jax.random.key(seed), 8)
    tokens = scatter_about(seeds[0], (TOKENS, D), 1.0, 6.0, ((0, 32), (1, 4)))
    cotangent = scatter_about(seeds[1], (TOKENS, D), 1.0, 6.0, ((0, 32), (1, 4)))
    routes_keys = jax.random.split(jax.random.fold_in(seeds[2], 1), TOKENS // TOK_DEV)
    routes_turns = jax.random.permutation(jax.random.fold_in(seeds[2], 3), TOKENS // TOK_DEV)
    routes = jax.vmap(lambda own, number: assign_block(jax.random.fold_in(seeds[2], 2), own, number, TOK_DEV, EXPERTS, TOP, CAP, 2))(routes_keys, routes_turns).reshape((TOKENS, TOP))
    gates = jnp.clip(0.2 + 0.8 * jax.random.uniform(seeds[3], (TOKENS, TOP), jnp.float32) ** steps_of(seeds[3], (TOKENS, TOP), ((0, 32),), -0.2, 0.2), 0.2, 1.0)
    w_gate = scatter_about(seeds[4], (EXPERTS, D, H), D ** -0.5, 0.0625, ((0, 32), (1, 4)))
    w_up = scatter_about(seeds[5], (EXPERTS, D, H), D ** -0.5, 0.0625, ((0, 32), (1, 4)))
    w_down = scatter_about(seeds[6], (EXPERTS, H, D), H ** -0.5, 0.1875, ((0, 32), (2, 4)))
    return {"tokens": tokens, "cotangent": cotangent, "routes": routes, "gates": gates, "w_gate": w_gate, "w_up": w_up, "w_down": w_down}


def block_ranks(picks):
    onehot = (picks[:, None] == jnp.arange(EXPERTS, dtype=jnp.int32)[None, :]).astype(jnp.int32)
    before = jnp.cumsum(onehot, axis=0) - onehot
    return jnp.sum(before * onehot, axis=1).astype(jnp.int32)


def part_sum(left_rows, weight):
    count = left_rows.shape[0]
    left_parts = left_rows.reshape(count, N_DP, D_PART).astype(jnp.float32)
    weight_parts = weight.reshape(N_DP, D_PART, weight.shape[1]).astype(jnp.float32)
    partial_value = jnp.einsum("rqd,qdh->rqh", left_parts, weight_parts)
    rounded = lax.optimization_barrier(partial_value.astype(jnp.bfloat16))
    return jnp.sum(rounded.astype(jnp.float32), axis=1)


def expert_work(operands):
    expert_x, expert_d, weight_gate, weight_up, weight_down = operands
    gate_pre = part_sum(expert_x, weight_gate)
    up_pre = part_sum(expert_x, weight_up)
    hidden = (jax.nn.silu(gate_pre) * up_pre).astype(jnp.bfloat16)
    out_rows = jnp.dot(hidden, weight_down, preferred_element_type=jnp.float32).astype(jnp.bfloat16)
    hidden_grad = part_sum(expert_d, weight_down.T)
    gate_sig = jax.nn.sigmoid(gate_pre)
    gate_grad = (hidden_grad * up_pre * gate_sig * (1.0 + gate_pre * (1.0 - gate_sig))).astype(jnp.bfloat16)
    up_grad = (hidden_grad * gate_pre * gate_sig).astype(jnp.bfloat16)
    row_grads = (jnp.dot(gate_grad, weight_gate.T, preferred_element_type=jnp.float32)
                 + jnp.dot(up_grad, weight_up.T, preferred_element_type=jnp.float32)).astype(jnp.bfloat16)
    grad_gate = jnp.dot(expert_x.T, gate_grad, preferred_element_type=jnp.float32).astype(jnp.bfloat16)
    grad_up = jnp.dot(expert_x.T, up_grad, preferred_element_type=jnp.float32).astype(jnp.bfloat16)
    grad_down = jnp.dot(hidden.T, expert_d, preferred_element_type=jnp.float32).astype(jnp.bfloat16)
    return out_rows, row_grads, grad_gate, grad_up, grad_down


def reference(tokens, cotangent, routes, gates, w_gate, w_up, w_down):
    picks = routes.reshape(N_EXPERT, TOK_DEV * TOP)
    slot_rank = jax.vmap(block_ranks)(picks).reshape(-1)
    expert_of = routes.reshape(-1).astype(jnp.int32)
    token_of = (jnp.arange(TOKENS * TOP, dtype=jnp.int32) // TOP).astype(jnp.int32)
    row_of = ((token_of // TOK_DEV) * CAP + slot_rank).astype(jnp.int32)
    gate_flat = gates.reshape(-1)
    x_rows = jnp.zeros((EXPERTS, ROWS, D), jnp.bfloat16).at[expert_of, row_of].set(tokens[token_of])
    weighted = (gate_flat[:, None] * cotangent[token_of].astype(jnp.float32)).astype(jnp.bfloat16)
    dout_rows = jnp.zeros((EXPERTS, ROWS, D), jnp.bfloat16).at[expert_of, row_of].set(weighted)
    out_rows, row_grads, grad_gate, grad_up, grad_down = lax.map(
        expert_work, (x_rows, dout_rows, w_gate, w_up, w_down))
    picked = out_rows[expert_of, row_of].astype(jnp.float32) * gate_flat[:, None]
    mixed = jnp.sum(picked.reshape(TOKENS, TOP, D), axis=1).astype(jnp.bfloat16)
    back = row_grads[expert_of, row_of].astype(jnp.float32)
    input_grad = jnp.sum(back.reshape(TOKENS, TOP, D), axis=1).astype(jnp.bfloat16)
    return mixed, input_grad, grad_gate, grad_up, grad_down
```

```python
import functools

import jax
import jax.numpy as jnp
from jax import lax
from jax.experimental import pallas as pl
from jax.experimental.pallas import tpu as pltpu
from jax.sharding import PartitionSpec as P

MESH = pl.DeviceIdType.MESH
BF = jnp.bfloat16
F32 = jnp.float32

TB = 128
TOP = 4
E = 32
CAP = 24
PAIR = 2 * CAP
D = 1792
HD = D // 2
H = 1024
ROWS = 768
NCH = 4
CH = ROWS // NCH
W3 = 3 * H
HW = W3 // 2
NN = (((1,), (0,)), ((), ()))
NT = (((1,), (1,)), ((), ()))
TN = (((0,), (0,)), ((), ()))


def mm(a, b, dims):
    return lax.dot_general(a, b, dims, preferred_element_type=F32)


def kernel(
    a1, a2, tok, cot, wg, wu, wd,
    mixed, ingrad, ogg, ogu, ogd,
    p1, p2, tokp, xd_send, xd_rows, part, r1, r2, act, or_send, or_recv, pt, res, vg, vu, vd,
    pair_s, pair_r, loc, wsem, ds_s, ds_r, x_s, x_r, cb_s, cb_r, fin_s, fin_r, fin_l, gsem,
):
    q = lax.axis_index("dp")
    e = lax.axis_index("expert")
    chip = e // 2
    core = e % 2
    other = 1 - core
    cz, cy = chip // 4, chip % 4
    right, left, opp = (q + 1) % 4, (q + 3) % 4, (q + 2) % 4
    partner = chip * 2 + other

    def to_chip(j):
        a, b = j // 4, j % 4
        return ((cz + a + b) % 4) * 4 + (cy + b) % 4

    def from_chip(j):
        a, b = j // 4, j % 4
        return ((cz + 8 - a - b) % 4) * 4 + (cy + 4 - b) % 4

    def half(c):
        return pl.ds(pl.multiple_of(c * HD, 128), HD)

    def rows48(j):
        return pl.ds(pl.multiple_of(j * PAIR, 16), PAIR)

    def blk(c):
        return pl.ds(pl.multiple_of(c * TB, TB), TB)

    local = [
        pltpu.make_async_copy(a1, p1.at[core], loc.at[0]),
        pltpu.make_async_copy(a2, p2.at[core], loc.at[1]),
        pltpu.make_async_copy(tok.at[:, half(core)], tokp.at[0, blk(core), :], loc.at[2]),
        pltpu.make_async_copy(cot.at[:, half(core)], tokp.at[1, blk(core), :], loc.at[3]),
    ]
    for cp in local:
        cp.start()

    bar = pltpu.get_barrier_semaphore()

    def greet(j, carry):
        d = to_chip(j)
        for k in range(2):
            pl.semaphore_signal(
                bar, inc=1, device_id={"dp": q, "expert": d * 2 + k}, device_id_type=MESH
            )
        return carry

    pl.semaphore_signal(bar, inc=1, device_id={"dp": q, "expert": partner}, device_id_type=MESH)
    for n in (right, left, opp):
        pl.semaphore_signal(bar, inc=1, device_id={"dp": n, "expert": e}, device_id_type=MESH)
    lax.fori_loop(1, 16, greet, 0)
    pl.semaphore_wait(bar, 34)

    def remote(src, dst, ss, rs, dp, ex):
        return pltpu.make_async_remote_copy(
            src_ref=src, dst_ref=dst, send_sem=ss, recv_sem=rs,
            device_id={"dp": dp, "expert": ex}, device_id_type=MESH,
        )

    def pair_copies(c):
        return [
            remote(a1, p1.at[c], pair_s.at[0], pair_r.at[0], q, partner),
            remote(a2, p2.at[c], pair_s.at[1], pair_r.at[1], q, partner),
            remote(tok.at[:, half(1 - c)], tokp.at[0, blk(c), :], pair_s.at[2], pair_r.at[2], q, partner),
            remote(cot.at[:, half(1 - c)], tokp.at[1, blk(c), :], pair_s.at[3], pair_r.at[3], q, partner),
        ]

    mine = pair_copies(core)
    for cp in mine:
        cp.start()
    weights = [
        pltpu.make_async_copy(wg, vg, wsem.at[0]),
        pltpu.make_async_copy(wu, vu, wsem.at[1]),
        pltpu.make_async_copy(wd, vd, wsem.at[2]),
    ]
    for cp in weights:
        cp.start()
    for cp in local:
        cp.wait()
    for cp in pair_copies(other):
        cp.wait_recv()

    def hits(row):
        return jnp.concatenate([p1[0, row : row + 1, :], p1[1, row : row + 1, :]], axis=1)

    def fill(j):
        d = to_chip(j)
        rid = (lax.broadcasted_iota(jnp.int32, (2 * PAIR, 2 * TB), 0) + d * (2 * PAIR)).astype(F32)
        one = jnp.zeros((2 * PAIR, 2 * TB), F32)
        gat = jnp.zeros((2 * PAIR, 2 * TB), F32)
        for k in range(TOP):
            hit = rid == hits(k)
            one = jnp.where(hit, 1.0, one)
            gat = jnp.where(hit, hits(8 + k), gat)
        xs = mm(one.astype(BF), tokp[0], NN).astype(BF)
        dsv = mm(gat.astype(BF), tokp[1], NN).astype(BF)
        xd_send[j, :, 0] = xs.reshape(2, PAIR, HD)
        xd_send[j, :, 1] = dsv.reshape(2, PAIR, HD)

    def disp(j, k, dst_chip, c_src):
        c_dst = core if k == 0 else other
        return remote(
            xd_send.at[j, c_dst], xd_rows.at[:, rows48(j), half(c_src)],
            ds_s.at[j, k], ds_r.at[j, k], q, dst_chip * 2 + c_dst,
        )

    fill(0)
    own = pltpu.make_async_copy(xd_send.at[0, core], xd_rows.at[:, rows48(0), half(core)], loc.at[4])
    own.start()
    disp(0, 1, chip, core).start()

    def send_one(j, carry):
        fill(j)
        d = to_chip(j)
        disp(j, 0, d, core).start()
        disp(j, 1, d, core).start()
        return carry

    lax.fori_loop(1, 16, send_one, 0)

    def build(n, carry):
        cols = pl.ds(pl.multiple_of(n * 256, 256), 256)
        cid = (lax.broadcasted_iota(jnp.int32, (TB, 256), 1) + n * 256).astype(F32)
        for b in range(2):
            one = jnp.zeros((TB, 256), F32)
            gat = jnp.zeros((TB, 256), F32)
            for k in range(TOP):
                hit = cid == p2[b, :, k : k + 1]
                one = jnp.where(hit, 1.0, one)
                gat = jnp.where(hit, p2[b, :, TOP + k : TOP + k + 1], gat)
            pt[0, b * TB : (b + 1) * TB, cols] = gat.astype(BF)
            pt[1, b * TB : (b + 1) * TB, cols] = one.astype(BF)
        return carry

    lax.fori_loop(0, E * PAIR // 256, build, 0)

    for cp in weights:
        cp.wait()

    def cols256(n):
        return pl.ds(pl.multiple_of(n * 256, 256), 256)

    def chunk(a):
        return pl.ds(a * CH, CH)

    def step_a(a):
        for j in range(4 * a, 4 * a + 4):
            if j == 0:
                own.wait()
            else:
                disp(j, 0, chip, core).wait_recv()
            disp(j, 1, chip, other).wait_recv()

        def body(n, carry):
            cs = cols256(n)
            x = xd_rows[0, chunk(a), :]
            part[a, :, :, cs] = mm(x, vg[:, cs], NN).astype(BF).reshape(4, PAIR, 256)
            part[a, :, :, pl.ds(pl.multiple_of(n * 256 + H, 256), 256)] = (
                mm(x, vu[:, cs], NN).astype(BF).reshape(4, PAIR, 256)
            )
            part[a, :, :, pl.ds(pl.multiple_of(n * 256 + 2 * H, 256), 256)] = (
                mm(xd_rows[1, chunk(a), :], vd[cs, :], NT).astype(BF).reshape(4, PAIR, 256)
            )
            return carry

        lax.fori_loop(0, H // 256, body, 0)
        for cp in rs1(a):
            cp.start()

    def rs1(a):
        return [
            remote(part.at[a, opp, :, pl.ds(0, HW)], r1.at[a, 0], x_s.at[a, 0], x_r.at[a, 0], right, e),
            remote(part.at[a, opp, :, pl.ds(HW, HW)], r1.at[a, 1], x_s.at[a, 1], x_r.at[a, 1], left, e),
        ]

    def rs2(a):
        return [
            remote(part.at[a, right], r2.at[a, 0], x_s.at[a, 2], x_r.at[a, 2], right, e),
            remote(part.at[a, left], r2.at[a, 1], x_s.at[a, 3], x_r.at[a, 3], left, e),
        ]

    def arow(a, n):
        return pl.ds(pl.multiple_of(a * CH + n * PAIR, 16), PAIR)

    def ag1(a, n):
        blkr = act.at[arow(a, n), :]
        return [
            remote(blkr, blkr, x_s.at[a, 4], x_r.at[a, 4], right, e),
            remote(blkr, blkr, x_s.at[a, 5], x_r.at[a, 5], left, e),
        ]

    def ag2(a, n0, n1):
        b0 = act.at[arow(a, n0), pl.ds(0, HW)]
        b1 = act.at[arow(a, n1), pl.ds(HW, HW)]
        return [
            remote(b0, b0, x_s.at[a, 6], x_r.at[a, 6], right, e),
            remote(b1, b1, x_s.at[a, 7], x_r.at[a, 7], left, e),
        ]

    def step_b(a):
        for cp in rs1(a):
            cp.wait_recv()
        s2 = rs2(a)
        part[a, right, :, 0:HW] = (part[a, right, :, 0:HW].astype(F32) + r1[a, 0].astype(F32)).astype(BF)
        s2[0].start()
        part[a, left, :, HW:W3] = (part[a, left, :, HW:W3].astype(F32) + r1[a, 1].astype(F32)).astype(BF)
        s2[1].start()

    def step_c(a):
        for cp in rs2(a):
            cp.wait_recv()

        def total(lo):
            s = slice(lo, lo + H)
            return part[a, q, :, s].astype(F32) + r2[a, 0, :, s].astype(F32) + r2[a, 1, :, s].astype(F32)

        g, u, hg = total(0), total(H), total(2 * H)
        sig = jax.nn.sigmoid(g)
        act[arow(a, q), 0:H] = (g * sig * u).astype(BF)
        act[arow(a, q), H : 2 * H] = (hg * u * sig * (1.0 + g * (1.0 - sig))).astype(BF)
        act[arow(a, q), 2 * H : W3] = (hg * g * sig).astype(BF)
        for cp in ag1(a, q):
            cp.start()

    def step_d(a):
        ag1(a, left)[0].wait_recv()
        ag1(a, right)[1].wait_recv()
        for cp in ag2(a, left, right):
            cp.start()

    def comb(j, k, dst_chip, src_e):
        c_dst = core if k == 0 else other
        return remote(
            or_send.at[:, rows48(j), half(c_dst)], or_recv.at[:, rows48(src_e), :],
            cb_s.at[j, k], cb_r.at[j, k], q, dst_chip * 2 + c_dst,
        )

    own_back = pltpu.make_async_copy(or_send.at[:, rows48(0), half(core)], or_recv.at[:, rows48(e), :], loc.at[5])

    def step_e(a):
        for cp in ag2(a, opp, opp):
            cp.wait_recv()

        def body(n, carry):
            cs = cols256(n)
            or_send[0, chunk(a), cs] = mm(act[chunk(a), 0:H], vd[:, cs], NN).astype(BF)
            or_send[1, chunk(a), cs] = (
                mm(act[chunk(a), H : 2 * H], vg[cs, :], NT) + mm(act[chunk(a), 2 * H : W3], vu[cs, :], NT)
            ).astype(BF)
            return carry

        lax.fori_loop(0, D // 256, body, 0)
        for j in range(4 * a, 4 * a + 4):
            d = from_chip(j)
            if j == 0:
                own_back.start()
            else:
                comb(j, 0, d, e).start()
            comb(j, 1, d, e).start()

    for step, a in (
        (step_a, 0), (step_b, 0), (step_c, 0), (step_a, 1), (step_d, 0), (step_b, 1), (step_e, 0), (step_c, 1),
        (step_a, 2), (step_d, 1), (step_b, 2), (step_e, 1), (step_c, 2), (step_a, 3), (step_d, 2), (step_b, 3),
        (step_e, 2), (step_c, 3), (step_d, 3), (step_e, 3),
    ):
        step(a)

    def grad_x(n, carry):
        cs = cols256(n)
        x = xd_rows[0, :, cs]
        vg[cs, :] = mm(x, act[:, H : 2 * H], TN).astype(BF)
        vu[cs, :] = mm(x, act[:, 2 * H : W3], TN).astype(BF)
        return carry

    lax.fori_loop(0, D // 256, grad_x, 0)
    out_w = [
        pltpu.make_async_copy(vg, ogg, gsem.at[0]),
        pltpu.make_async_copy(vu, ogu, gsem.at[1]),
        pltpu.make_async_copy(vd, ogd, gsem.at[2]),
    ]
    out_w[0].start()
    out_w[1].start()

    def grad_d(n, carry):
        cs = cols256(n)
        vd[cs, :] = mm(act[:, cs], xd_rows[1], TN).astype(BF)
        return carry

    lax.fori_loop(0, H // 256, grad_d, 0)
    out_w[2].start()

    def arrived(j, carry):
        src = to_chip(j)
        comb(j, 0, chip, src * 2 + core).wait_recv()
        comb(j, 1, chip, src * 2 + other).wait_recv()
        return carry

    own_back.wait()
    comb(0, 1, chip, chip * 2 + other).wait_recv()
    lax.fori_loop(1, 16, arrived, 0)
    res[0] = mm(pt[0], or_recv[0], NN).astype(BF)
    res[1] = mm(pt[1], or_recv[1], NN).astype(BF)
    fin = []
    for k, out in enumerate((mixed, ingrad)):
        away = remote(res.at[k, blk(other), :], out.at[:, half(core)], fin_s.at[k], fin_r.at[k], q, partner)
        here = pltpu.make_async_copy(res.at[k, blk(core), :], out.at[:, half(core)], fin_l.at[k])
        away.start()
        here.start()
        fin.append((away, here))

    for cp in mine:
        cp.wait_send()
    disp(0, 1, chip, core).wait_send()
    comb(0, 1, chip, e).wait_send()

    def sent(j, carry):
        for k in range(2):
            disp(j, k, chip, core).wait_send()
            comb(j, k, chip, e).wait_send()
        return carry

    lax.fori_loop(1, 16, sent, 0)
    for a in range(NCH):
        for cp in rs1(a) + rs2(a) + ag1(a, q) + ag2(a, left, right):
            cp.wait_send()
    for cp in out_w:
        cp.wait()
    for k, out in enumerate((mixed, ingrad)):
        fin[k][0].wait_send()
        fin[k][1].wait()
        remote(res.at[k, blk(core), :], out.at[:, half(other)], fin_s.at[k], fin_r.at[k], q, partner).wait_recv()


def local(tokens, cotangent, routes, gates, w_gate, w_up, w_down):
    core = lax.axis_index("expert") % 2
    ids = jnp.arange(E, dtype=jnp.int32)
    onehot = routes[:, :, None] == ids[None, None, :]
    named = jnp.any(onehot, axis=1).astype(BF)
    tri = (jnp.arange(TB)[:, None] > jnp.arange(TB)[None, :]).astype(BF)
    before = jnp.dot(tri, named, preferred_element_type=F32)
    slot = jnp.sum(jnp.where(onehot, before[:, None, :], 0.0), axis=2)
    target = routes.astype(F32) * PAIR + slot + (core * CAP).astype(F32)
    a2 = jnp.pad(jnp.concatenate([target, gates], axis=1), ((0, 0), (0, 128 - 2 * TOP)))
    pad = jnp.zeros((4, TB), F32)
    a1 = jnp.concatenate([target.T, pad, gates.T, pad], axis=0)

    any_spec = pl.BlockSpec(memory_space=pl.ANY)
    dma = pltpu.SemaphoreType.DMA
    out = pl.pallas_call(
        kernel,
        out_shape=(
            jax.ShapeDtypeStruct((TB, D), BF),
            jax.ShapeDtypeStruct((TB, D), BF),
            jax.ShapeDtypeStruct((D, H), BF),
            jax.ShapeDtypeStruct((D, H), BF),
            jax.ShapeDtypeStruct((H, D), BF),
        ),
        in_specs=[any_spec] * 7,
        out_specs=[any_spec] * 5,
        scratch_shapes=[
            pltpu.VMEM((2, 16, TB), F32),
            pltpu.VMEM((2, TB, 128), F32),
            pltpu.VMEM((2, 2 * TB, HD), BF),
            pltpu.VMEM((16, 2, 2, PAIR, HD), BF),
            pltpu.VMEM((2, ROWS, D), BF),
            pltpu.VMEM((NCH, 4, PAIR, W3), BF),
            pltpu.VMEM((NCH, 2, PAIR, HW), BF),
            pltpu.VMEM((NCH, 2, PAIR, W3), BF),
            pltpu.VMEM((ROWS, W3), BF),
            pltpu.VMEM((2, ROWS, D), BF),
            pltpu.VMEM((2, E * PAIR, HD), BF),
            pltpu.VMEM((2, 2 * TB, E * PAIR), BF),
            pltpu.VMEM((2, 2 * TB, HD), BF),
            pltpu.VMEM((D, H), BF),
            pltpu.VMEM((D, H), BF),
            pltpu.VMEM((H, D), BF),
            dma((4,)), dma((4,)), dma((6,)), dma((3,)),
            dma((16, 2)), dma((16, 2)), dma((NCH, 8)), dma((NCH, 8)),
            dma((16, 2)), dma((16, 2)), dma((2,)), dma((2,)), dma((2,)), dma((3,)),
        ],
        compiler_params=pltpu.CompilerParams(
            collective_id=0, has_side_effects=True, vmem_limit_bytes=62 * 1024 * 1024
        ),
    )(a1, a2, tokens, cotangent, w_gate.reshape(D, H), w_up.reshape(D, H), w_down.reshape(H, D))
    mixed, ingrad, gg, gu, gd = out
    return mixed, ingrad, gg[None], gu[None], gd[None]


def solution(mesh):
    in_specs = (
        P("expert", "dp"),
        P("expert", "dp"),
        P("expert", None),
        P("expert", None),
        P("expert", "dp", None),
        P("expert", "dp", None),
        P("expert", None, "dp"),
    )
    out_specs = (
        P("expert", "dp"),
        P("expert", "dp"),
        P("expert", "dp", None),
        P("expert", "dp", None),
        P("expert", None, "dp"),
    )
    return jax.shard_map(local, mesh=mesh, in_specs=in_specs, out_specs=out_specs, check_vma=False)
```

```python
import functools

import jax
import jax.numpy as jnp
from jax import lax
from jax.experimental import pallas as pl
from jax.experimental.pallas import tpu as pltpu
from jax.sharding import PartitionSpec as P

MESH = pl.DeviceIdType.MESH
BF = jnp.bfloat16
F32 = jnp.float32

TB = 128
TOP = 4
E = 32
CAP = 24
PAIR = 2 * CAP
D = 1792
HD = D // 2
H = 1024
ROWS = 768
NCH = 4
CH = ROWS // NCH
W3 = 3 * H
HW = W3 // 2
SLOTS = (
    (0, 0), (1, 1), (1, 3), (3, 1),
    (1, 2), (2, 1), (2, 3), (3, 2),
    (3, 3), (2, 2), (0, 2), (2, 0),
    (0, 1), (1, 0), (0, 3), (3, 0),
)
NN = (((1,), (0,)), ((), ()))
NT = (((1,), (1,)), ((), ()))
TN = (((0,), (0,)), ((), ()))


def mm(a, b, dims):
    return lax.dot_general(a, b, dims, preferred_element_type=F32)


def kernel(
    routes, gates, tok, cot, wg, wu, wd,
    mixed, ingrad, ogg, ogu, ogd,
    p1, tokp, xd_send, xd_rows, part, r1, r2, act, or_send, or_recv, pt, res, vg, vu, vd,
    pair_s, pair_r, loc, wsem, ag_s, ag_r, ds_s, ds_r, x_s, x_r, cb_s, cb_r, fin_s, fin_r, fin_l, gsem,
):
    q = lax.axis_index("dp")
    e = lax.axis_index("expert")
    chip = e // 2
    core = e % 2
    other = 1 - core
    cz, cy = chip // 4, chip % 4
    right, left, opp = (q + 1) % 4, (q + 3) % 4, (q + 2) % 4
    partner = chip * 2 + other

    flip = core == 1
    pa, pb = jnp.where(flip, cy, cz), jnp.where(flip, cz, cy)

    def chip_at(a, b):
        a, b = a % 4, b % 4
        return jnp.where(flip, b * 4 + a, a * 4 + b)

    def slot(a, b):
        return jnp.where(flip, SLOTS.index((b, a)), SLOTS.index((a, b)))

    def to_chip(j):
        dz, dy = SLOTS[j]
        return ((cz + dz) % 4) * 4 + (cy + dy) % 4

    def from_chip(j):
        dz, dy = SLOTS[j]
        return ((cz + 4 - dz) % 4) * 4 + (cy + 4 - dy) % 4

    def half(c):
        return pl.ds(pl.multiple_of(c * HD, 128), HD)

    def rows48(j):
        return pl.ds(pl.multiple_of(j * PAIR, 16), PAIR)

    def blk(c):
        return pl.ds(pl.multiple_of(c * TB, TB), TB)

    local = [
        pltpu.make_async_copy(tok.at[:, half(core)], tokp.at[0, 0, blk(core), :], loc.at[2]),
        pltpu.make_async_copy(cot.at[:, half(core)], tokp.at[0, 1, blk(core), :], loc.at[3]),
    ]
    for cp in local:
        cp.start()

    bar = pltpu.get_barrier_semaphore()

    def greet(d, carry):
        @pl.when(d != e)
        def _():
            pl.semaphore_signal(bar, inc=1, device_id={"dp": q, "expert": d}, device_id_type=MESH)

        return carry

    for n in (right, left, opp):
        pl.semaphore_signal(bar, inc=1, device_id={"dp": n, "expert": e}, device_id_type=MESH)
    lax.fori_loop(0, E, greet, 0)
    pl.semaphore_wait(bar, 34)

    def remote(src, dst, ss, rs, dp, ex):
        return pltpu.make_async_remote_copy(
            src_ref=src, dst_ref=dst, send_sem=ss, recv_sem=rs,
            device_id={"dp": dp, "expert": ex}, device_id_type=MESH,
        )

    def pair_copies(c):
        return [
            remote(tok.at[:, half(1 - c)], tokp.at[0, 0, blk(c), :], pair_s.at[2], pair_r.at[2], q, partner),
            remote(cot.at[:, half(1 - c)], tokp.at[0, 1, blk(c), :], pair_s.at[3], pair_r.at[3], q, partner),
        ]

    def pair_rows(c):
        return remote(p1.at[0, c], p1.at[0, c], pair_s.at[0], pair_r.at[0], q, partner)

    mine = pair_copies(core)
    for cp in mine:
        cp.start()

    ids = lax.broadcasted_iota(jnp.int32, (E, TB), 0)
    picks = [routes[k : k + 1, :] == ids for k in range(TOP)]
    named = functools.reduce(jnp.logical_or, picks)
    earlier = lax.broadcasted_iota(jnp.int32, (TB, TB), 0) < lax.broadcasted_iota(jnp.int32, (TB, TB), 1)
    before = mm(jnp.where(named, 1.0, 0.0).astype(BF), jnp.where(earlier, 1.0, 0.0).astype(BF), NN)
    first = (core * CAP).astype(F32)
    for k in range(TOP):
        rank = jnp.sum(jnp.where(picks[k], before, 0.0), axis=0, keepdims=True)
        p1[0, core, k : k + 1, :] = routes[k : k + 1, :].astype(F32) * PAIR + rank + first
        p1[0, core, TOP + k : TOP + k + 1, :] = gates[k : k + 1, :]
    pair_rows(core).start()
    weights = [
        pltpu.make_async_copy(wg, vg, wsem.at[0]),
        pltpu.make_async_copy(wu, vu, wsem.at[1]),
        pltpu.make_async_copy(wd, vd, wsem.at[2]),
    ]
    for cp in weights:
        cp.start()
    for cp in local:
        cp.wait()
    for cp in pair_copies(other) + [pair_rows(other)]:
        cp.wait_recv()

    def spread(a):
        d = chip_at(pa + a, pb) * 2 + core
        return [
            remote(p1.at[0], p1.at[a], ag_s.at[a, 0], ag_r.at[a, 0], q, d),
            remote(tokp.at[0], tokp.at[a], ag_s.at[a, 1], ag_r.at[a, 1], q, d),
        ]

    for a in (1, 3, 2):
        for cp in spread(a):
            cp.start()

    def fill(a, b):
        d = chip_at(pa, pb + b)
        rid = (lax.broadcasted_iota(jnp.int32, (2 * PAIR, 2 * TB), 0) + d * (2 * PAIR)).astype(F32)
        one = jnp.zeros((2 * PAIR, 2 * TB), F32)
        gat = jnp.zeros((2 * PAIR, 2 * TB), F32)

        def of(row):
            return jnp.concatenate([p1[a, 0, row : row + 1, :], p1[a, 1, row : row + 1, :]], axis=1)

        for k in range(TOP):
            hit = rid == of(k)
            one = jnp.where(hit, 1.0, one)
            gat = jnp.where(hit, of(TOP + k), gat)
        xs = mm(one.astype(BF), tokp[a, 0], NN).astype(BF)
        dsv = mm(gat.astype(BF), tokp[a, 1], NN).astype(BF)
        xd_send[4 * a + b, :, 0] = xs.reshape(2, PAIR, HD)
        xd_send[4 * a + b, :, 1] = dsv.reshape(2, PAIR, HD)

    def disp(a, b, k):
        c_dst = core if k == 0 else other
        j = slot(a, b)
        src, dst = xd_send.at[4 * a + b, c_dst], xd_rows.at[:, rows48(j), half(core)]
        if b == 0 and k == 0:
            return pltpu.make_async_copy(src, dst, ds_r.at[j, 0])
        return remote(src, dst, ds_s.at[j, k], ds_r.at[j, k], q, chip_at(pa, pb + b) * 2 + c_dst)

    def from_other(a, b):
        j = slot(a, b)
        return remote(
            xd_send.at[4 * a + b, core], xd_rows.at[:, rows48(j), half(other)],
            ds_s.at[j, 1], ds_r.at[j, 1], q, partner,
        )

    have = {0}

    def send_chunk(c):
        for a, b in sorted(SLOTS[4 * c : 4 * c + 4], key=lambda ab: (0, 1, 3, 2)[ab[0]]):
            if a not in have:
                have.add(a)
                for cp in spread(a):
                    cp.wait_recv()
            fill(a, b)
            disp(a, b, 0).start()
            disp(a, b, 1).start()

    for c in range(NCH):
        send_chunk(c)

    def build(n, carry):
        r = pl.ds(pl.multiple_of(n * 128, 128), 128)
        rid = (lax.broadcasted_iota(jnp.int32, (128, TB), 0) + n * 128).astype(F32)
        for b in range(2):
            one = jnp.zeros((128, TB), F32)
            gat = jnp.zeros((128, TB), F32)
            for k in range(TOP):
                hit = rid == p1[0, b, k : k + 1, :]
                one = jnp.where(hit, 1.0, one)
                gat = jnp.where(hit, p1[0, b, TOP + k : TOP + k + 1, :], gat)
            pt[0, r, b * TB : (b + 1) * TB] = gat.astype(BF)
            pt[1, r, b * TB : (b + 1) * TB] = one.astype(BF)
        return carry

    lax.fori_loop(0, E * PAIR // 128, build, 0)

    for cp in weights:
        cp.wait()

    def cols256(n):
        return pl.ds(pl.multiple_of(n * 256, 256), 256)

    def chunk(a):
        return pl.ds(a * CH, CH)

    def step_a(a):
        for sa, sb in SLOTS[4 * a : 4 * a + 4]:
            mine_in = disp(sa, sb, 0)
            if sb == 0:
                mine_in.wait()
            else:
                mine_in.wait_recv()
            from_other(sa, sb).wait_recv()

        def body(n, carry):
            cs = cols256(n)
            x = xd_rows[0, chunk(a), :]
            part[a, :, :, cs] = mm(x, vg[:, cs], NN).astype(BF).reshape(4, PAIR, 256)
            part[a, :, :, pl.ds(pl.multiple_of(n * 256 + H, 256), 256)] = (
                mm(x, vu[:, cs], NN).astype(BF).reshape(4, PAIR, 256)
            )
            part[a, :, :, pl.ds(pl.multiple_of(n * 256 + 2 * H, 256), 256)] = (
                mm(xd_rows[1, chunk(a), :], vd[cs, :], NT).astype(BF).reshape(4, PAIR, 256)
            )
            return carry

        lax.fori_loop(0, H // 256, body, 0)
        for cp in rs1(a):
            cp.start()

    def rs1(a):
        return [
            remote(part.at[a, opp, :, pl.ds(0, HW)], r1.at[a, 0], x_s.at[a, 0], x_r.at[a, 0], right, e),
            remote(part.at[a, opp, :, pl.ds(HW, HW)], r1.at[a, 1], x_s.at[a, 1], x_r.at[a, 1], left, e),
        ]

    def rs2(a):
        return [
            remote(part.at[a, right], r2.at[a, 0], x_s.at[a, 2], x_r.at[a, 2], right, e),
            remote(part.at[a, left], r2.at[a, 1], x_s.at[a, 3], x_r.at[a, 3], left, e),
        ]

    def arow(a, n):
        return pl.ds(pl.multiple_of(a * CH + n * PAIR, 16), PAIR)

    def ag1(a, n):
        blkr = act.at[arow(a, n), :]
        return [
            remote(blkr, blkr, x_s.at[a, 4], x_r.at[a, 4], right, e),
            remote(blkr, blkr, x_s.at[a, 5], x_r.at[a, 5], left, e),
        ]

    def ag2(a, n0, n1):
        b0 = act.at[arow(a, n0), pl.ds(0, HW)]
        b1 = act.at[arow(a, n1), pl.ds(HW, HW)]
        return [
            remote(b0, b0, x_s.at[a, 6], x_r.at[a, 6], right, e),
            remote(b1, b1, x_s.at[a, 7], x_r.at[a, 7], left, e),
        ]

    def step_b(a):
        for cp in rs1(a):
            cp.wait_recv()
        s2 = rs2(a)
        part[a, right, :, 0:HW] = (part[a, right, :, 0:HW].astype(F32) + r1[a, 0].astype(F32)).astype(BF)
        s2[0].start()
        part[a, left, :, HW:W3] = (part[a, left, :, HW:W3].astype(F32) + r1[a, 1].astype(F32)).astype(BF)
        s2[1].start()

    def step_c(a):
        for cp in rs2(a):
            cp.wait_recv()

        def total(lo):
            s = slice(lo, lo + H)
            return part[a, q, :, s].astype(F32) + r2[a, 0, :, s].astype(F32) + r2[a, 1, :, s].astype(F32)

        g, u, hg = total(0), total(H), total(2 * H)
        sig = jax.nn.sigmoid(g)
        act[arow(a, q), 0:H] = (g * sig * u).astype(BF)
        act[arow(a, q), H : 2 * H] = (hg * u * sig * (1.0 + g * (1.0 - sig))).astype(BF)
        act[arow(a, q), 2 * H : W3] = (hg * g * sig).astype(BF)
        for cp in ag1(a, q):
            cp.start()

    def step_d(a):
        ag1(a, left)[0].wait_recv()
        ag1(a, right)[1].wait_recv()
        for cp in ag2(a, left, right):
            cp.start()

    def comb(j, k, dst_chip, src_e):
        c_dst = core if k == 0 else other
        return remote(
            or_send.at[:, rows48(j), half(c_dst)], or_recv.at[:, rows48(src_e), :],
            cb_s.at[j, k], cb_r.at[j, k], q, dst_chip * 2 + c_dst,
        )

    own_back = pltpu.make_async_copy(or_send.at[:, rows48(0), half(core)], or_recv.at[:, rows48(e), :], loc.at[5])

    def step_e(a):
        for cp in ag2(a, opp, opp):
            cp.wait_recv()

        def body(n, carry):
            cs = cols256(n)
            or_send[0, chunk(a), cs] = mm(act[chunk(a), 0:H], vd[:, cs], NN).astype(BF)
            or_send[1, chunk(a), cs] = (
                mm(act[chunk(a), H : 2 * H], vg[cs, :], NT) + mm(act[chunk(a), 2 * H : W3], vu[cs, :], NT)
            ).astype(BF)
            return carry

        lax.fori_loop(0, D // 256, body, 0)
        for j in range(4 * a, 4 * a + 4):
            d = from_chip(j)
            if j == 0:
                own_back.start()
            else:
                comb(j, 0, d, e).start()
            comb(j, 1, d, e).start()

    for step, a in (
        (step_a, 0), (step_b, 0), (step_c, 0), (step_a, 1), (step_d, 0), (step_b, 1), (step_e, 0), (step_c, 1),
        (step_a, 2), (step_d, 1), (step_b, 2), (step_e, 1), (step_c, 2), (step_a, 3), (step_d, 2), (step_b, 3),
        (step_e, 2), (step_c, 3), (step_d, 3), (step_e, 3),
    ):
        step(a)

    def grad_x(n, carry):
        cs = cols256(n)
        x = xd_rows[0, :, cs]
        vg[cs, :] = mm(x, act[:, H : 2 * H], TN).astype(BF)
        vu[cs, :] = mm(x, act[:, 2 * H : W3], TN).astype(BF)
        return carry

    lax.fori_loop(0, D // 256, grad_x, 0)
    out_w = [
        pltpu.make_async_copy(vg, ogg, gsem.at[0]),
        pltpu.make_async_copy(vu, ogu, gsem.at[1]),
        pltpu.make_async_copy(vd, ogd, gsem.at[2]),
    ]
    out_w[0].start()
    out_w[1].start()

    def grad_d(n, carry):
        cs = cols256(n)
        vd[cs, :] = mm(act[:, cs], xd_rows[1], TN).astype(BF)
        return carry

    lax.fori_loop(0, H // 256, grad_d, 0)
    out_w[2].start()

    own_back.wait()
    for j in range(16):
        src = to_chip(j)
        if j > 0:
            comb(j, 0, chip, src * 2 + core).wait_recv()
        comb(j, 1, chip, src * 2 + other).wait_recv()
    res[0] = mm(pt[0], or_recv[0], TN).astype(BF)
    res[1] = mm(pt[1], or_recv[1], TN).astype(BF)
    fin = []
    for k, out in enumerate((mixed, ingrad)):
        away = remote(res.at[k, blk(other), :], out.at[:, half(core)], fin_s.at[k], fin_r.at[k], q, partner)
        here = pltpu.make_async_copy(res.at[k, blk(core), :], out.at[:, half(core)], fin_l.at[k])
        away.start()
        here.start()
        fin.append((away, here))

    for cp in mine + [pair_rows(core)]:
        cp.wait_send()
    for a in (1, 2, 3):
        for cp in spread(a):
            cp.wait_send()
    for a, b in SLOTS:
        if b != 0:
            disp(a, b, 0).wait_send()
        disp(a, b, 1).wait_send()
    for j in range(16):
        if j > 0:
            comb(j, 0, chip, e).wait_send()
        comb(j, 1, chip, e).wait_send()
    for a in range(NCH):
        for cp in rs1(a) + rs2(a) + ag1(a, q) + ag2(a, left, right):
            cp.wait_send()
    for cp in out_w:
        cp.wait()
    for k, out in enumerate((mixed, ingrad)):
        fin[k][0].wait_send()
        fin[k][1].wait()
        remote(res.at[k, blk(core), :], out.at[:, half(other)], fin_s.at[k], fin_r.at[k], q, partner).wait_recv()


def settle(i0, i1, i2, i3, i4, o0, o1, o2, o3, o4, b0, b1, b2, b3, b4, in_s, out_s):
    loads, stores = [], []
    for n, (i, b, o) in enumerate(zip((i2, i3, i4, i0, i1), (b2, b3, b4, b0, b1), (o2, o3, o4, o0, o1))):
        step = i.shape[0] // 4
        for k in range(4):
            r = pl.ds(k * step, step)
            loads.append(pltpu.make_async_copy(i.at[r, :], b.at[r, :], in_s.at[n, k]))
            stores.append(pltpu.make_async_copy(b.at[r, :], o.at[r, :], out_s.at[n, k]))
    for cp in loads:
        cp.start()
    for cp, st in zip(loads, stores):
        cp.wait()
        st.start()
    for st in stores:
        st.wait()


def local(tokens, cotangent, routes, gates, w_gate, w_up, w_down):
    vmem = pl.BlockSpec(memory_space=pltpu.VMEM)
    any_spec = pl.BlockSpec(memory_space=pl.ANY)
    dma = pltpu.SemaphoreType.DMA
    out = pl.pallas_call(
        kernel,
        out_shape=(
            jax.ShapeDtypeStruct((TB, D), BF),
            jax.ShapeDtypeStruct((TB, D), BF),
            jax.ShapeDtypeStruct((D, H), BF),
            jax.ShapeDtypeStruct((D, H), BF),
            jax.ShapeDtypeStruct((H, D), BF),
        ),
        in_specs=[vmem] * 2 + [any_spec] * 5,
        out_specs=[any_spec] * 5,
        scratch_shapes=[
            pltpu.VMEM((4, 2, 2 * TOP, TB), F32),
            pltpu.VMEM((4, 2, 2 * TB, HD), BF),
            pltpu.VMEM((16, 2, 2, PAIR, HD), BF),
            pltpu.VMEM((2, ROWS, D), BF),
            pltpu.VMEM((NCH, 4, PAIR, W3), BF),
            pltpu.VMEM((NCH, 2, PAIR, HW), BF),
            pltpu.VMEM((NCH, 2, PAIR, W3), BF),
            pltpu.VMEM((ROWS, W3), BF),
            pltpu.VMEM((2, ROWS, D), BF),
            pltpu.VMEM((2, E * PAIR, HD), BF),
            pltpu.VMEM((2, E * PAIR, 2 * TB), BF),
            pltpu.VMEM((2, 2 * TB, HD), BF),
            pltpu.VMEM((D, H), BF),
            pltpu.VMEM((D, H), BF),
            pltpu.VMEM((H, D), BF),
            dma((4,)), dma((4,)), dma((6,)), dma((3,)), dma((4, 2)), dma((4, 2)),
            dma((16, 2)), dma((16, 2)), dma((NCH, 8)), dma((NCH, 8)),
            dma((16, 2)), dma((16, 2)), dma((2,)), dma((2,)), dma((2,)), dma((3,)),
        ],
        compiler_params=pltpu.CompilerParams(
            collective_id=0, has_side_effects=True, vmem_limit_bytes=62 * 1024 * 1024
        ),
    )(routes.T, gates.T, tokens, cotangent, w_gate.reshape(D, H), w_up.reshape(D, H), w_down.reshape(H, D))
    mixed, ingrad, gg, gu, gd = pl.pallas_call(
        settle,
        out_shape=[jax.ShapeDtypeStruct(o.shape, o.dtype) for o in out],
        in_specs=[pl.BlockSpec(memory_space=pltpu.HBM)] * 5,
        out_specs=[any_spec] * 5,
        scratch_shapes=[pltpu.VMEM((TB, D), BF), pltpu.VMEM((TB, D), BF), pltpu.VMEM((D, H), BF), pltpu.VMEM((D, H), BF), pltpu.VMEM((H, D), BF), dma((5, 4)), dma((5, 4))],
        compiler_params=pltpu.CompilerParams(vmem_limit_bytes=60 * 1024 * 1024),
    )(*out)
    return mixed, ingrad, gg[None], gu[None], gd[None]


def solution(mesh):
    in_specs = (
        P("expert", "dp"),
        P("expert", "dp"),
        P("expert", None),
        P("expert", None),
        P("expert", "dp", None),
        P("expert", "dp", None),
        P("expert", None, "dp"),
    )
    out_specs = (
        P("expert", "dp"),
        P("expert", "dp"),
        P("expert", "dp", None),
        P("expert", "dp", None),
        P("expert", None, "dp"),
    )
    return jax.shard_map(local, mesh=mesh, in_specs=in_specs, out_specs=out_specs, check_vma=False)
```

```python
import functools

import jax
import jax.numpy as jnp
from jax import lax
from jax.experimental import pallas as pl
from jax.experimental.pallas import tpu as pltpu
from jax.sharding import PartitionSpec as P

MESH = pl.DeviceIdType.MESH
BF = jnp.bfloat16
F32 = jnp.float32

TB = 128
TOP = 4
E = 32
CAP = 24
PAIR = 2 * CAP
D = 1792
HD = D // 2
H = 1024
ROWS = 768
Q = H // 4
SLOTS = (
    (1, 1), (1, 3), (3, 1), (1, 2), (2, 1), (0, 2), (2, 0),
    (2, 2), (3, 3), (2, 3), (3, 2), (0, 1), (1, 0), (0, 3), (3, 0), (0, 0),
)
SIZES = (3, 4, 4, 4, 1)
FIRST = tuple(sum(SIZES[:n]) for n in range(len(SIZES)))
NCH = len(SIZES)
NN = (((1,), (0,)), ((), ()))
NT = (((1,), (1,)), ((), ()))
TN = (((0,), (0,)), ((), ()))


def mm(a, b, dims):
    return lax.dot_general(a, b, dims, preferred_element_type=F32)


def kernel(
    routes, gates, tok, cot, wg, wu, wd,
    mixed, ingrad, ogg, ogu, ogd,
    p1, tokp, xd_send, xd_rows, part, r1, r2, act, or_send, or_recv, pt, res, cmb, vg, vu, vd,
    pair_s, pair_r, loc, wsem, ag_s, ag_r, ds_s, ds_r, x_s, x_r, cb_s, cb_r, gv_s, gv_r, fin_s, fin_r, fin_l, gsem,
):
    q = lax.axis_index("dp")
    e = lax.axis_index("expert")
    chip = e // 2
    core = e % 2
    other = 1 - core
    cz, cy = chip // 4, chip % 4
    right, left, opp = (q + 1) % 4, (q + 3) % 4, (q + 2) % 4
    partner = chip * 2 + other

    flip = core == 1
    pa, pb = jnp.where(flip, cy, cz), jnp.where(flip, cz, cy)

    def chip_at(a, b):
        a, b = a % 4, b % 4
        return jnp.where(flip, b * 4 + a, a * 4 + b)

    def slot(a, b):
        return jnp.where(flip, SLOTS.index((b, a)), SLOTS.index((a, b)))

    def half(c):
        return pl.ds(pl.multiple_of(c * HD, 128), HD)

    def rows48(j):
        return pl.ds(pl.multiple_of(j * PAIR, 16), PAIR)

    def blk(c):
        return pl.ds(pl.multiple_of(c * TB, TB), TB)

    local = [
        pltpu.make_async_copy(tok.at[:, half(core)], tokp.at[0, 0, blk(core), :], loc.at[2]),
        pltpu.make_async_copy(cot.at[:, half(core)], tokp.at[0, 1, blk(core), :], loc.at[3]),
    ]
    for cp in local:
        cp.start()

    bar = pltpu.get_barrier_semaphore()

    def greet(d, carry):
        @pl.when(d != e)
        def _():
            pl.semaphore_signal(bar, inc=1, device_id={"dp": q, "expert": d}, device_id_type=MESH)

        return carry

    for n in (right, left, opp):
        pl.semaphore_signal(bar, inc=1, device_id={"dp": n, "expert": e}, device_id_type=MESH)
    lax.fori_loop(0, E, greet, 0)
    pl.semaphore_wait(bar, 34)

    def remote(src, dst, ss, rs, dp, ex):
        return pltpu.make_async_remote_copy(
            src_ref=src, dst_ref=dst, send_sem=ss, recv_sem=rs,
            device_id={"dp": dp, "expert": ex}, device_id_type=MESH,
        )

    def pair_copies(c):
        return [
            remote(tok.at[:, half(1 - c)], tokp.at[0, 0, blk(c), :], pair_s.at[2], pair_r.at[2], q, partner),
            remote(cot.at[:, half(1 - c)], tokp.at[0, 1, blk(c), :], pair_s.at[3], pair_r.at[3], q, partner),
        ]

    def pair_rows(c):
        return remote(p1.at[0, c], p1.at[0, c], pair_s.at[0], pair_r.at[0], q, partner)

    mine = pair_copies(core)
    for cp in mine:
        cp.start()

    ids = lax.broadcasted_iota(jnp.int32, (E, TB), 0)
    picks = [routes[k : k + 1, :] == ids for k in range(TOP)]
    named = functools.reduce(jnp.logical_or, picks)
    earlier = lax.broadcasted_iota(jnp.int32, (TB, TB), 0) < lax.broadcasted_iota(jnp.int32, (TB, TB), 1)
    before = mm(jnp.where(named, 1.0, 0.0).astype(BF), jnp.where(earlier, 1.0, 0.0).astype(BF), NN)
    first = (core * CAP).astype(F32)
    for k in range(TOP):
        rank = jnp.sum(jnp.where(picks[k], before, 0.0), axis=0, keepdims=True)
        p1[0, core, k : k + 1, :] = routes[k : k + 1, :].astype(F32) * PAIR + rank + first
        p1[0, core, TOP + k : TOP + k + 1, :] = gates[k : k + 1, :]
    pair_rows(core).start()
    weights = [
        pltpu.make_async_copy(wg, vg, wsem.at[0]),
        pltpu.make_async_copy(wu, vu, wsem.at[1]),
        pltpu.make_async_copy(wd, vd, wsem.at[2]),
    ]
    for cp in weights:
        cp.start()
    for cp in local:
        cp.wait()
    for cp in pair_copies(other) + [pair_rows(other)]:
        cp.wait_recv()

    def spread(a):
        d = chip_at(pa + a, pb) * 2 + core
        return [
            remote(p1.at[0], p1.at[a], ag_s.at[a, 0], ag_r.at[a, 0], q, d),
            remote(tokp.at[0], tokp.at[a], ag_s.at[a, 1], ag_r.at[a, 1], q, d),
        ]

    def step_s(a):
        for cp in spread(a):
            cp.start()

    for a in (1, 3, 2):
        step_s(a)

    def group(a, b):
        return pl.ds((4 * a + b) * 2 * PAIR, 2 * PAIR)

    def fill(a, b):
        d = chip_at(pa, pb + b)
        rid = (lax.broadcasted_iota(jnp.int32, (2 * PAIR, 2 * TB), 0) + d * (2 * PAIR)).astype(F32)
        one = jnp.zeros((2 * PAIR, 2 * TB), F32)
        gat = jnp.zeros((2 * PAIR, 2 * TB), F32)

        def of(row):
            return jnp.concatenate([p1[a, 0, row : row + 1, :], p1[a, 1, row : row + 1, :]], axis=1)

        for k in range(TOP):
            hit = rid == of(k)
            one = jnp.where(hit, 1.0, one)
            gat = jnp.where(hit, of(TOP + k), gat)
        one, gat = one.astype(BF), gat.astype(BF)
        pt[0, group(a, b)] = gat
        pt[1, group(a, b)] = one
        xs = mm(one, tokp[a, 0], NN).astype(BF)
        dsv = mm(gat, tokp[a, 1], NN).astype(BF)
        xd_send[4 * a + b, :, 0] = xs.reshape(2, PAIR, HD)
        xd_send[4 * a + b, :, 1] = dsv.reshape(2, PAIR, HD)

    def disp(a, b, k):
        c_dst = core if k == 0 else other
        j = slot(a, b)
        src, dst = xd_send.at[4 * a + b, c_dst], xd_rows.at[:, rows48(j), half(core)]
        if b == 0 and k == 0:
            return pltpu.make_async_copy(src, dst, ds_r.at[j, 0])
        return remote(src, dst, ds_s.at[j, k], ds_r.at[j, k], q, chip_at(pa, pb + b) * 2 + c_dst)

    def from_other(a, b):
        j = slot(a, b)
        return remote(
            xd_send.at[4 * a + b, core], xd_rows.at[:, rows48(j), half(other)],
            ds_s.at[j, 1], ds_r.at[j, 1], q, partner,
        )

    have = {0}

    def step_f(c):
        for a, b in sorted(SLOTS[FIRST[c] : FIRST[c] + SIZES[c]], key=lambda ab: (0, 1, 3, 2)[ab[0]]):
            if a not in have:
                have.add(a)
                for cp in spread(a):
                    cp.wait_recv()
            fill(a, b)
            disp(a, b, 0).start()
            disp(a, b, 1).start()

    def step_w(a):
        for cp in weights:
            cp.wait()

    def cols256(n):
        return pl.ds(pl.multiple_of(n * 256, 256), 256)

    def chunk(a):
        return pl.ds(FIRST[a] * PAIR, SIZES[a] * PAIR)

    def step_a(a):
        for sa, sb in SLOTS[FIRST[a] : FIRST[a] + SIZES[a]]:
            mine_in = disp(sa, sb, 0)
            if sb == 0:
                mine_in.wait()
            else:
                mine_in.wait_recv()
            from_other(sa, sb).wait_recv()

        def body(i, carry):
            cs = cols256((q + 2 + i) % 4)
            x = xd_rows[0, chunk(a), :]
            part[0, chunk(a), cs] = mm(x, vg[:, cs], NN).astype(BF)
            part[1, chunk(a), cs] = mm(x, vu[:, cs], NN).astype(BF)
            part[2, chunk(a), cs] = mm(xd_rows[1, chunk(a), :], vd[cs, :], NT).astype(BF)
            return carry

        body(0, 0)
        for cp in rs1(a):
            cp.start()
        lax.fori_loop(1, 4, body, 0)

    def cols(n):
        return pl.ds(pl.multiple_of(n * Q, Q), Q)

    def lower(n):
        return pl.ds(pl.multiple_of(n * Q, 128), Q // 2)

    def upper(n):
        return pl.ds(pl.multiple_of(n * Q + Q // 2, 128), Q // 2)

    def rs1(a):
        return [
            remote(part.at[:, chunk(a), lower(opp)], r1.at[0, :, chunk(a), :], x_s.at[a, 0], x_r.at[a, 0], right, e),
            remote(part.at[:, chunk(a), upper(opp)], r1.at[1, :, chunk(a), :], x_s.at[a, 1], x_r.at[a, 1], left, e),
        ]

    def rs2(a):
        return [
            remote(part.at[:, chunk(a), cols(right)], r2.at[0, :, chunk(a), :], x_s.at[a, 2], x_r.at[a, 2], right, e),
            remote(part.at[:, chunk(a), cols(left)], r2.at[1, :, chunk(a), :], x_s.at[a, 3], x_r.at[a, 3], left, e),
        ]

    def ag1(a, n):
        own = act.at[:, chunk(a), cols(n)]
        return [
            remote(own, own, x_s.at[a, 4], x_r.at[a, 4], right, e),
            remote(own, own, x_s.at[a, 5], x_r.at[a, 5], left, e),
        ]

    def ag2(a, n0, n1):
        b0 = act.at[:, chunk(a), lower(n0)]
        b1 = act.at[:, chunk(a), upper(n1)]
        return [
            remote(b0, b0, x_s.at[a, 6], x_r.at[a, 6], right, e),
            remote(b1, b1, x_s.at[a, 7], x_r.at[a, 7], left, e),
        ]

    def step_b(a):
        for cp in rs1(a):
            cp.wait_recv()
        s2 = rs2(a)
        part[:, chunk(a), lower(right)] = (part[:, chunk(a), lower(right)].astype(F32) + r1[0, :, chunk(a), :].astype(F32)).astype(BF)
        s2[0].start()
        part[:, chunk(a), upper(left)] = (part[:, chunk(a), upper(left)].astype(F32) + r1[1, :, chunk(a), :].astype(F32)).astype(BF)
        s2[1].start()

    def step_c(a):
        for cp in rs2(a):
            cp.wait_recv()

        def total(k):
            return part[k, chunk(a), cols(q)].astype(F32) + r2[0, k, chunk(a), :].astype(F32) + r2[1, k, chunk(a), :].astype(F32)

        g, u, hg = total(0), total(1), total(2)
        sig = jax.nn.sigmoid(g)
        act[0, chunk(a), cols(q)] = (g * sig * u).astype(BF)
        act[1, chunk(a), cols(q)] = (hg * u * sig * (1.0 + g * (1.0 - sig))).astype(BF)
        act[2, chunk(a), cols(q)] = (hg * g * sig).astype(BF)
        for cp in ag1(a, q):
            cp.start()

    def step_d(a):
        ag1(a, left)[0].wait_recv()
        ag1(a, right)[1].wait_recv()
        for cp in ag2(a, left, right):
            cp.start()

    def comb(a, b, k):
        rows = rows48(slot(a, b))
        n = 4 * a + b if k == 0 else 4 * b + a
        dst = or_recv.at[:, pl.ds(pl.multiple_of(n * 2 * PAIR + core * PAIR, 16), PAIR), :]
        if k == 0:
            src = or_send.at[:, rows, half(core)]
            if b == 0:
                return pltpu.make_async_copy(src, dst, cb_r.at[n, 0])
            return remote(src, dst, cb_s.at[n, 0], cb_r.at[n, 0], q, chip_at(pa, pb + 4 - b) * 2 + core)
        src = or_send.at[:, rows, half(other)]
        return remote(src, dst, cb_s.at[n, 1], cb_r.at[n, 1], q, chip_at(pa + 4 - a, pb) * 2 + other)

    def comb_other(a, b):
        n = 4 * a + b
        dst = or_recv.at[:, pl.ds(pl.multiple_of(n * 2 * PAIR + other * PAIR, 16), PAIR), :]
        return remote(or_send.at[:, rows48(0), half(core)], dst, cb_s.at[n, 1], cb_r.at[n, 1], q, partner)

    def give(a):
        return remote(tokp.at[a], cmb.at[a - 1], gv_s.at[a], gv_r.at[a], q, chip_at(pa + 4 - a, pb) * 2 + core)

    def added(a, k):
        r = pl.ds(a * 8 * PAIR, 8 * PAIR)
        return mm(pt[k, r, :], or_recv[k, r, :], TN)

    def step_g(a):
        for b in range(4):
            cp = comb(a, b, 0)
            if b == 0:
                cp.wait()
            else:
                cp.wait_recv()
            comb_other(a, b).wait_recv()
        if a != 0:
            for k in range(2):
                tokp[a, k] = added(a, k).astype(BF)
            give(a).start()

    def step_e(a):
        for cp in ag2(a, opp, opp):
            cp.wait_recv()

        def body(n, carry):
            cs = cols256(n)
            or_send[0, chunk(a), cs] = mm(act[0, chunk(a), :], vd[:, cs], NN).astype(BF)
            or_send[1, chunk(a), cs] = (
                mm(act[1, chunk(a), :], vg[cs, :], NT) + mm(act[2, chunk(a), :], vu[cs, :], NT)
            ).astype(BF)
            return carry

        lax.fori_loop(0, D // 256, body, 0)
        for sa, sb in SLOTS[FIRST[a] : FIRST[a] + SIZES[a]]:
            comb(sa, sb, 0).start()
            comb(sa, sb, 1).start()

    for step, a in (
        (step_f, 0), (step_f, 1), (step_f, 2), (step_w, 0), (step_a, 0), (step_f, 3), (step_b, 0), (step_f, 4), (step_a, 1), (step_c, 0), (step_b, 1), (step_d, 0), (step_a, 2), (step_c, 1), (step_e, 0), (step_b, 2), (step_d, 1), (step_a, 3), (step_c, 2), (step_e, 1), (step_b, 3), (step_d, 2), (step_a, 4), (step_c, 3), (step_e, 2), (step_b, 4), (step_d, 3), (step_c, 4), (step_e, 3), (step_g, 2), (step_d, 4), (step_g, 1), (step_g, 3), (step_e, 4),
    ):
        step(a)

    def grad_x(n, carry):
        cs = cols256(n)
        x = xd_rows[0, :, cs]
        vg[cs, :] = mm(x, act[1], TN).astype(BF)
        vu[cs, :] = mm(x, act[2], TN).astype(BF)
        return carry

    lax.fori_loop(0, D // 256, grad_x, 0)
    out_w = [
        pltpu.make_async_copy(vg, ogg, gsem.at[0]),
        pltpu.make_async_copy(vu, ogu, gsem.at[1]),
        pltpu.make_async_copy(vd, ogd, gsem.at[2]),
    ]
    out_w[0].start()
    out_w[1].start()

    def grad_d(n, carry):
        cs = cols256(n)
        vd[cs, :] = mm(act[0, :, cs], xd_rows[1], TN).astype(BF)
        return carry

    lax.fori_loop(0, H // 256, grad_d, 0)
    out_w[2].start()

    step_g(0)
    for a in (2, 1, 3):
        give(a).wait_recv()
    for k in range(2):
        far = cmb[0, k].astype(F32) + cmb[1, k].astype(F32) + cmb[2, k].astype(F32)
        res[k] = (added(0, k) + far).astype(BF)
    fin = []
    for k, out in enumerate((mixed, ingrad)):
        away = remote(res.at[k, blk(other), :], out.at[:, half(core)], fin_s.at[k], fin_r.at[k], q, partner)
        here = pltpu.make_async_copy(res.at[k, blk(core), :], out.at[:, half(core)], fin_l.at[k])
        away.start()
        here.start()
        fin.append((away, here))

    for cp in mine + [pair_rows(core)]:
        cp.wait_send()
    for a in (1, 2, 3):
        for cp in spread(a):
            cp.wait_send()
    for a, b in SLOTS:
        if b != 0:
            disp(a, b, 0).wait_send()
        disp(a, b, 1).wait_send()
    for a, b in SLOTS:
        if b != 0:
            comb(a, b, 0).wait_send()
        comb(a, b, 1).wait_send()
    for a in (1, 2, 3):
        give(a).wait_send()
    for a in range(NCH):
        for cp in rs1(a) + rs2(a) + ag1(a, q) + ag2(a, left, right):
            cp.wait_send()
    for cp in out_w:
        cp.wait()
    for k, out in enumerate((mixed, ingrad)):
        fin[k][0].wait_send()
        fin[k][1].wait()
        remote(res.at[k, blk(core), :], out.at[:, half(other)], fin_s.at[k], fin_r.at[k], q, partner).wait_recv()


def settle(i0, i1, i2, i3, i4, o0, o1, o2, o3, o4, b0, b1, b2, b3, b4, in_s, out_s):
    loads, stores = [], []
    for n, (i, b, o) in enumerate(zip((i2, i3, i4, i0, i1), (b2, b3, b4, b0, b1), (o2, o3, o4, o0, o1))):
        step = i.shape[0] // 4
        for k in range(4):
            r = pl.ds(k * step, step)
            loads.append(pltpu.make_async_copy(i.at[r, :], b.at[r, :], in_s.at[n, k]))
            stores.append(pltpu.make_async_copy(b.at[r, :], o.at[r, :], out_s.at[n, k]))
    for cp in loads:
        cp.start()
    for cp, st in zip(loads, stores):
        cp.wait()
        st.start()
    for st in stores:
        st.wait()


def local(tokens, cotangent, routes, gates, w_gate, w_up, w_down):
    vmem = pl.BlockSpec(memory_space=pltpu.VMEM)
    any_spec = pl.BlockSpec(memory_space=pl.ANY)
    dma = pltpu.SemaphoreType.DMA
    out = pl.pallas_call(
        kernel,
        out_shape=(
            jax.ShapeDtypeStruct((TB, D), BF),
            jax.ShapeDtypeStruct((TB, D), BF),
            jax.ShapeDtypeStruct((D, H), BF),
            jax.ShapeDtypeStruct((D, H), BF),
            jax.ShapeDtypeStruct((H, D), BF),
        ),
        in_specs=[vmem] * 2 + [any_spec] * 5,
        out_specs=[any_spec] * 5,
        scratch_shapes=[
            pltpu.VMEM((4, 2, 2 * TOP, TB), F32),
            pltpu.VMEM((4, 2, 2 * TB, HD), BF),
            pltpu.VMEM((16, 2, 2, PAIR, HD), BF),
            pltpu.VMEM((2, ROWS, D), BF),
            pltpu.VMEM((3, ROWS, H), BF),
            pltpu.VMEM((2, 3, ROWS, Q // 2), BF),
            pltpu.VMEM((2, 3, ROWS, Q), BF),
            pltpu.VMEM((3, ROWS, H), BF),
            pltpu.VMEM((2, ROWS, D), BF),
            pltpu.VMEM((2, E * PAIR, HD), BF),
            pltpu.VMEM((2, E * PAIR, 2 * TB), BF),
            pltpu.VMEM((2, 2 * TB, HD), BF),
            pltpu.VMEM((3, 2, 2 * TB, HD), BF),
            pltpu.VMEM((D, H), BF),
            pltpu.VMEM((D, H), BF),
            pltpu.VMEM((H, D), BF),
            dma((4,)), dma((4,)), dma((6,)), dma((3,)), dma((4, 2)), dma((4, 2)),
            dma((16, 2)), dma((16, 2)), dma((NCH, 8)), dma((NCH, 8)),
            dma((16, 2)), dma((16, 2)), dma((4,)), dma((4,)), dma((2,)), dma((2,)), dma((2,)), dma((3,)),
        ],
        compiler_params=pltpu.CompilerParams(
            collective_id=0, has_side_effects=True, vmem_limit_bytes=62 * 1024 * 1024
        ),
    )(routes.T, gates.T, tokens, cotangent, w_gate.reshape(D, H), w_up.reshape(D, H), w_down.reshape(H, D))
    mixed, ingrad, gg, gu, gd = pl.pallas_call(
        settle,
        out_shape=[jax.ShapeDtypeStruct(o.shape, o.dtype) for o in out],
        in_specs=[pl.BlockSpec(memory_space=pltpu.HBM)] * 5,
        out_specs=[any_spec] * 5,
        scratch_shapes=[pltpu.VMEM((TB, D), BF), pltpu.VMEM((TB, D), BF), pltpu.VMEM((D, H), BF), pltpu.VMEM((D, H), BF), pltpu.VMEM((H, D), BF), dma((5, 4)), dma((5, 4))],
        compiler_params=pltpu.CompilerParams(vmem_limit_bytes=60 * 1024 * 1024),
    )(*out)
    return mixed, ingrad, gg[None], gu[None], gd[None]


def solution(mesh):
    in_specs = (
        P("expert", "dp"),
        P("expert", "dp"),
        P("expert", None),
        P("expert", None),
        P("expert", "dp", None),
        P("expert", "dp", None),
        P("expert", None, "dp"),
    )
    out_specs = (
        P("expert", "dp"),
        P("expert", "dp"),
        P("expert", "dp", None),
        P("expert", "dp", None),
        P("expert", None, "dp"),
    )
    return jax.shard_map(local, mesh=mesh, in_specs=in_specs, out_specs=out_specs, check_vma=False)
```

```python
import functools

import jax
import jax.numpy as jnp
from jax import lax
from jax.experimental import pallas as pl
from jax.experimental.pallas import tpu as pltpu
from jax.sharding import PartitionSpec as P

MESH = pl.DeviceIdType.MESH
BF = jnp.bfloat16
F32 = jnp.float32

TB = 128
TOP = 4
E = 32
CAP = 24
PAIR = 2 * CAP
D = 1792
HD = D // 2
H = 1024
ROWS = 768
Q = H // 4
SLOTS = (
    (1, 1), (1, 3), (3, 1), (1, 2), (2, 1), (0, 2), (2, 0),
    (2, 2), (3, 3), (2, 3), (3, 2), (0, 1), (1, 0), (0, 3), (3, 0), (0, 0),
)
SIZES = (3, 4, 4, 4, 1)
FIRST = tuple(sum(SIZES[:n]) for n in range(len(SIZES)))
NCH = len(SIZES)
NN = (((1,), (0,)), ((), ()))
NT = (((1,), (1,)), ((), ()))
TN = (((0,), (0,)), ((), ()))


def mm(a, b, dims):
    return lax.dot_general(a, b, dims, preferred_element_type=F32)


def kernel(
    routes, gates, tok, cot, wg, wu, wd,
    mixed, ingrad, ogg, ogu, ogd,
    p1, tokp, xd_send, xd_rows, part, r1, r2, act, or_send, or_recv, pt, res, cmb, vg, vu, vd,
    pair_s, pair_r, loc, wsem, ag_s, ag_r, ds_s, ds_r, x_s, x_r, cb_s, cb_r, gv_s, gv_r, fin_s, fin_r, fin_l, gsem,
):
    q = lax.axis_index("dp")
    e = lax.axis_index("expert")
    chip = e // 2
    core = e % 2
    other = 1 - core
    cz, cy = chip // 4, chip % 4
    right, left, opp = (q + 1) % 4, (q + 3) % 4, (q + 2) % 4
    partner = chip * 2 + other

    flip = core == 1
    pa, pb = jnp.where(flip, cy, cz), jnp.where(flip, cz, cy)

    def chip_at(a, b):
        a, b = a % 4, b % 4
        return jnp.where(flip, b * 4 + a, a * 4 + b)

    def slot(a, b):
        return jnp.where(flip, SLOTS.index((b, a)), SLOTS.index((a, b)))

    def half(c):
        return pl.ds(pl.multiple_of(c * HD, 128), HD)

    def rows48(j):
        return pl.ds(pl.multiple_of(j * PAIR, 16), PAIR)

    def blk(c):
        return pl.ds(pl.multiple_of(c * TB, TB), TB)

    local = [
        pltpu.make_async_copy(tok.at[:, half(core)], tokp.at[0, 0, blk(core), :], loc.at[2]),
        pltpu.make_async_copy(cot.at[:, half(core)], tokp.at[0, 1, blk(core), :], loc.at[3]),
    ]
    for cp in local:
        cp.start()

    bar = pltpu.get_barrier_semaphore()

    def greet(d, carry):
        @pl.when(d != e)
        def _():
            pl.semaphore_signal(bar, inc=1, device_id={"dp": q, "expert": d}, device_id_type=MESH)

        return carry

    for n in (right, left, opp):
        pl.semaphore_signal(bar, inc=1, device_id={"dp": n, "expert": e}, device_id_type=MESH)
    lax.fori_loop(0, E, greet, 0)
    pl.semaphore_wait(bar, 34)

    def remote(src, dst, ss, rs, dp, ex):
        return pltpu.make_async_remote_copy(
            src_ref=src, dst_ref=dst, send_sem=ss, recv_sem=rs,
            device_id={"dp": dp, "expert": ex}, device_id_type=MESH,
        )

    def pair_copies(c):
        return [
            remote(tok.at[:, half(1 - c)], tokp.at[0, 0, blk(c), :], pair_s.at[2], pair_r.at[2], q, partner),
            remote(cot.at[:, half(1 - c)], tokp.at[0, 1, blk(c), :], pair_s.at[3], pair_r.at[3], q, partner),
        ]

    def pair_rows(c):
        return remote(p1.at[0, c], p1.at[0, c], pair_s.at[0], pair_r.at[0], q, partner)

    mine = pair_copies(core)
    for cp in mine:
        cp.start()

    ids = lax.broadcasted_iota(jnp.int32, (E, TB), 0)
    picks = [routes[k : k + 1, :] == ids for k in range(TOP)]
    named = functools.reduce(jnp.logical_or, picks)
    earlier = lax.broadcasted_iota(jnp.int32, (TB, TB), 0) < lax.broadcasted_iota(jnp.int32, (TB, TB), 1)
    before = mm(jnp.where(named, 1.0, 0.0).astype(BF), jnp.where(earlier, 1.0, 0.0).astype(BF), NN)
    first = (core * CAP).astype(F32)
    for k in range(TOP):
        rank = jnp.sum(jnp.where(picks[k], before, 0.0), axis=0, keepdims=True)
        p1[0, core, k : k + 1, :] = routes[k : k + 1, :].astype(F32) * PAIR + rank + first
        p1[0, core, TOP + k : TOP + k + 1, :] = gates[k : k + 1, :]
    pair_rows(core).start()
    weights = [
        pltpu.make_async_copy(wg, vg, wsem.at[0]),
        pltpu.make_async_copy(wu, vu, wsem.at[1]),
        pltpu.make_async_copy(wd, vd, wsem.at[2]),
    ]
    for cp in weights:
        cp.start()
    for cp in local:
        cp.wait()
    for cp in pair_copies(other) + [pair_rows(other)]:
        cp.wait_recv()

    def spread(a):
        if a == 2:
            up, down = chip_at(pa + 1, pb) * 2 + core, chip_at(pa + 3, pb) * 2 + core
            return [
                remote(p1.at[1], p1.at[2], ag_s.at[2, 0], ag_r.at[2, 0], q, up),
                remote(tokp.at[1, 0], tokp.at[2, 0], ag_s.at[2, 1], ag_r.at[2, 1], q, up),
                remote(tokp.at[3, 1], tokp.at[2, 1], ag_s.at[2, 2], ag_r.at[2, 2], q, down),
            ]
        d = chip_at(pa + a, pb) * 2 + core
        return [
            remote(p1.at[0], p1.at[a], ag_s.at[a, 0], ag_r.at[a, 0], q, d),
            remote(tokp.at[0], tokp.at[a], ag_s.at[a, 1], ag_r.at[a, 1], q, d),
        ]

    def step_s(a):
        for cp in spread(a):
            cp.start()

    for a in (1, 3):
        step_s(a)

    def group(a, b):
        return pl.ds((4 * a + b) * 2 * PAIR, 2 * PAIR)

    def fill(a, b):
        d = chip_at(pa, pb + b)
        rid = (lax.broadcasted_iota(jnp.int32, (2 * PAIR, 2 * TB), 0) + d * (2 * PAIR)).astype(F32)
        one = jnp.zeros((2 * PAIR, 2 * TB), F32)
        gat = jnp.zeros((2 * PAIR, 2 * TB), F32)

        def of(row):
            return jnp.concatenate([p1[a, 0, row : row + 1, :], p1[a, 1, row : row + 1, :]], axis=1)

        for k in range(TOP):
            hit = rid == of(k)
            one = jnp.where(hit, 1.0, one)
            gat = jnp.where(hit, of(TOP + k), gat)
        one, gat = one.astype(BF), gat.astype(BF)
        pt[0, group(a, b)] = gat
        pt[1, group(a, b)] = one
        xs = mm(one, tokp[a, 0], NN).astype(BF)
        dsv = mm(gat, tokp[a, 1], NN).astype(BF)
        xd_send[4 * a + b, :, 0] = xs.reshape(2, PAIR, HD)
        xd_send[4 * a + b, :, 1] = dsv.reshape(2, PAIR, HD)

    def disp(a, b, k):
        c_dst = core if k == 0 else other
        j = slot(a, b)
        src, dst = xd_send.at[4 * a + b, c_dst], xd_rows.at[:, rows48(j), half(core)]
        if b == 0 and k == 0:
            return pltpu.make_async_copy(src, dst, ds_r.at[j, 0])
        return remote(src, dst, ds_s.at[j, k], ds_r.at[j, k], q, chip_at(pa, pb + b) * 2 + c_dst)

    def from_other(a, b):
        j = slot(a, b)
        return remote(
            xd_send.at[4 * a + b, core], xd_rows.at[:, rows48(j), half(other)],
            ds_s.at[j, 1], ds_r.at[j, 1], q, partner,
        )

    have = {0}

    def step_f(c):
        for a, b in sorted(SLOTS[FIRST[c] : FIRST[c] + SIZES[c]], key=lambda ab: (0, 1, 3, 2)[ab[0]]):
            if a not in have:
                have.add(a)
                for cp in spread(a):
                    cp.wait_recv()
            fill(a, b)
            disp(a, b, 0).start()
            disp(a, b, 1).start()

    def step_w(a):
        for cp in weights:
            cp.wait()

    def cols256(n):
        return pl.ds(pl.multiple_of(n * 256, 256), 256)

    def chunk(a):
        return pl.ds(FIRST[a] * PAIR, SIZES[a] * PAIR)

    def step_a(a):
        for sa, sb in SLOTS[FIRST[a] : FIRST[a] + SIZES[a]]:
            mine_in = disp(sa, sb, 0)
            if sb == 0:
                mine_in.wait()
            else:
                mine_in.wait_recv()
            from_other(sa, sb).wait_recv()

        def body(i, carry):
            cs = cols256((q + 2 + i) % 4)
            x = xd_rows[0, chunk(a), :]
            part[0, chunk(a), cs] = mm(x, vg[:, cs], NN).astype(BF)
            part[1, chunk(a), cs] = mm(x, vu[:, cs], NN).astype(BF)
            part[2, chunk(a), cs] = mm(xd_rows[1, chunk(a), :], vd[cs, :], NT).astype(BF)
            return carry

        body(0, 0)
        for cp in rs1(a):
            cp.start()
        lax.fori_loop(1, 4, body, 0)

    def cols(n):
        return pl.ds(pl.multiple_of(n * Q, Q), Q)

    def lower(n):
        return pl.ds(pl.multiple_of(n * Q, 128), Q // 2)

    def upper(n):
        return pl.ds(pl.multiple_of(n * Q + Q // 2, 128), Q // 2)

    def rs1(a):
        return [
            remote(part.at[:, chunk(a), lower(opp)], r1.at[0, :, chunk(a), :], x_s.at[a, 0], x_r.at[a, 0], right, e),
            remote(part.at[:, chunk(a), upper(opp)], r1.at[1, :, chunk(a), :], x_s.at[a, 1], x_r.at[a, 1], left, e),
        ]

    def rs2(a):
        return [
            remote(part.at[:, chunk(a), cols(right)], r2.at[0, :, chunk(a), :], x_s.at[a, 2], x_r.at[a, 2], right, e),
            remote(part.at[:, chunk(a), cols(left)], r2.at[1, :, chunk(a), :], x_s.at[a, 3], x_r.at[a, 3], left, e),
        ]

    def ag1(a, n):
        own = act.at[:, chunk(a), cols(n)]
        return [
            remote(own, own, x_s.at[a, 4], x_r.at[a, 4], right, e),
            remote(own, own, x_s.at[a, 5], x_r.at[a, 5], left, e),
        ]

    def ag2(a, n0, n1):
        b0 = act.at[:, chunk(a), lower(n0)]
        b1 = act.at[:, chunk(a), upper(n1)]
        return [
            remote(b0, b0, x_s.at[a, 6], x_r.at[a, 6], right, e),
            remote(b1, b1, x_s.at[a, 7], x_r.at[a, 7], left, e),
        ]

    def step_b(a):
        for cp in rs1(a):
            cp.wait_recv()
        s2 = rs2(a)
        part[:, chunk(a), lower(right)] = (part[:, chunk(a), lower(right)].astype(F32) + r1[0, :, chunk(a), :].astype(F32)).astype(BF)
        s2[0].start()
        part[:, chunk(a), upper(left)] = (part[:, chunk(a), upper(left)].astype(F32) + r1[1, :, chunk(a), :].astype(F32)).astype(BF)
        s2[1].start()

    def step_c(a):
        for cp in rs2(a):
            cp.wait_recv()

        def total(k):
            return part[k, chunk(a), cols(q)].astype(F32) + r2[0, k, chunk(a), :].astype(F32) + r2[1, k, chunk(a), :].astype(F32)

        g, u, hg = total(0), total(1), total(2)
        sig = jax.nn.sigmoid(g)
        act[0, chunk(a), cols(q)] = (g * sig * u).astype(BF)
        act[1, chunk(a), cols(q)] = (hg * u * sig * (1.0 + g * (1.0 - sig))).astype(BF)
        act[2, chunk(a), cols(q)] = (hg * g * sig).astype(BF)
        for cp in ag1(a, q):
            cp.start()

    def step_d(a):
        ag1(a, left)[0].wait_recv()
        ag1(a, right)[1].wait_recv()
        for cp in ag2(a, left, right):
            cp.start()

    def comb(a, b, k):
        rows = rows48(slot(a, b))
        n = 4 * a + b if k == 0 else 4 * b + a
        dst = or_recv.at[:, pl.ds(pl.multiple_of(n * 2 * PAIR + core * PAIR, 16), PAIR), :]
        if k == 0:
            src = or_send.at[:, rows, half(core)]
            if b == 0:
                return pltpu.make_async_copy(src, dst, cb_r.at[n, 0])
            return remote(src, dst, cb_s.at[n, 0], cb_r.at[n, 0], q, chip_at(pa, pb + 4 - b) * 2 + core)
        src = or_send.at[:, rows, half(other)]
        return remote(src, dst, cb_s.at[n, 1], cb_r.at[n, 1], q, chip_at(pa + 4 - a, pb) * 2 + other)

    def comb_other(a, b):
        n = 4 * a + b
        dst = or_recv.at[:, pl.ds(pl.multiple_of(n * 2 * PAIR + other * PAIR, 16), PAIR), :]
        return remote(or_send.at[:, rows48(0), half(core)], dst, cb_s.at[n, 1], cb_r.at[n, 1], q, partner)

    def give_far():
        down, up = chip_at(pa + 3, pb) * 2 + core, chip_at(pa + 1, pb) * 2 + core
        return [
            remote(tokp.at[2, 0], cmb.at[1, 0], gv_s.at[0], gv_r.at[0], q, down),
            remote(tokp.at[2, 1], cmb.at[1, 1], gv_s.at[2], gv_r.at[2], q, up),
        ]

    def give(a):
        return remote(tokp.at[a], cmb.at[a - 1], gv_s.at[a], gv_r.at[a], q, chip_at(pa + 4 - a, pb) * 2 + core)

    def added(a, k):
        r = pl.ds(a * 8 * PAIR, 8 * PAIR)
        return mm(pt[k, r, :], or_recv[k, r, :], TN)

    def step_g(a):
        if a == 2:
            for cp in spread(2):
                cp.wait_send()
        for b in range(4):
            cp = comb(a, b, 0)
            if b == 0:
                cp.wait()
            else:
                cp.wait_recv()
            comb_other(a, b).wait_recv()
        if a == 0:
            return
        passing = {1: 0, 3: 1}.get(a)
        for k in range(2):
            sums = added(a, k)
            if k == passing:
                give_far()[k].wait_recv()
                sums = sums + cmb[1, k].astype(F32)
            tokp[a, k] = sums.astype(BF)
        for cp in give_far() if a == 2 else [give(a)]:
            cp.start()

    def step_e(a):
        for cp in ag2(a, opp, opp):
            cp.wait_recv()

        def body(n, carry):
            cs = cols256(n)
            or_send[0, chunk(a), cs] = mm(act[0, chunk(a), :], vd[:, cs], NN).astype(BF)
            or_send[1, chunk(a), cs] = (
                mm(act[1, chunk(a), :], vg[cs, :], NT) + mm(act[2, chunk(a), :], vu[cs, :], NT)
            ).astype(BF)
            return carry

        lax.fori_loop(0, D // 256, body, 0)
        for sa, sb in SLOTS[FIRST[a] : FIRST[a] + SIZES[a]]:
            comb(sa, sb, 0).start()
            comb(sa, sb, 1).start()

    for step, a in (
        (step_f, 0), (step_s, 2), (step_f, 1), (step_f, 2), (step_w, 0), (step_a, 0), (step_f, 3), (step_b, 0), (step_f, 4), (step_a, 1), (step_c, 0), (step_b, 1), (step_d, 0), (step_a, 2), (step_c, 1), (step_e, 0), (step_b, 2), (step_d, 1), (step_a, 3), (step_c, 2), (step_e, 1), (step_b, 3), (step_d, 2), (step_a, 4), (step_c, 3), (step_e, 2), (step_b, 4), (step_d, 3), (step_c, 4), (step_e, 3), (step_g, 2), (step_d, 4), (step_g, 1), (step_g, 3), (step_e, 4),
    ):
        step(a)

    def grad_x(n, carry):
        cs = cols256(n)
        x = xd_rows[0, :, cs]
        vg[cs, :] = mm(x, act[1], TN).astype(BF)
        vu[cs, :] = mm(x, act[2], TN).astype(BF)
        return carry

    lax.fori_loop(0, D // 256, grad_x, 0)
    out_w = [
        pltpu.make_async_copy(vg, ogg, gsem.at[0]),
        pltpu.make_async_copy(vu, ogu, gsem.at[1]),
        pltpu.make_async_copy(vd, ogd, gsem.at[2]),
    ]
    out_w[0].start()
    out_w[1].start()

    def grad_d(n, carry):
        cs = cols256(n)
        vd[cs, :] = mm(act[0, :, cs], xd_rows[1], TN).astype(BF)
        return carry

    lax.fori_loop(0, H // 256, grad_d, 0)
    out_w[2].start()

    step_g(0)
    for a in (1, 3):
        give(a).wait_recv()
    for k in range(2):
        far = cmb[0, k].astype(F32) + cmb[2, k].astype(F32)
        res[k] = (added(0, k) + far).astype(BF)
    fin = []
    for k, out in enumerate((mixed, ingrad)):
        away = remote(res.at[k, blk(other), :], out.at[:, half(core)], fin_s.at[k], fin_r.at[k], q, partner)
        here = pltpu.make_async_copy(res.at[k, blk(core), :], out.at[:, half(core)], fin_l.at[k])
        away.start()
        here.start()
        fin.append((away, here))

    for cp in mine + [pair_rows(core)]:
        cp.wait_send()
    for a in (1, 3):
        for cp in spread(a):
            cp.wait_send()
    for a, b in SLOTS:
        if b != 0:
            disp(a, b, 0).wait_send()
        disp(a, b, 1).wait_send()
    for a, b in SLOTS:
        if b != 0:
            comb(a, b, 0).wait_send()
        comb(a, b, 1).wait_send()
    for cp in [give(1), give(3)] + give_far():
        cp.wait_send()
    for a in range(NCH):
        for cp in rs1(a) + rs2(a) + ag1(a, q) + ag2(a, left, right):
            cp.wait_send()
    for cp in out_w:
        cp.wait()
    for k, out in enumerate((mixed, ingrad)):
        fin[k][0].wait_send()
        fin[k][1].wait()
        remote(res.at[k, blk(core), :], out.at[:, half(other)], fin_s.at[k], fin_r.at[k], q, partner).wait_recv()


def settle(i0, i1, i2, i3, i4, o0, o1, o2, o3, o4, b0, b1, b2, b3, b4, in_s, out_s):
    loads, stores = [], []
    for n, (i, b, o) in enumerate(zip((i2, i3, i4, i0, i1), (b2, b3, b4, b0, b1), (o2, o3, o4, o0, o1))):
        step = i.shape[0] // 4
        for k in range(4):
            r = pl.ds(k * step, step)
            loads.append(pltpu.make_async_copy(i.at[r, :], b.at[r, :], in_s.at[n, k]))
            stores.append(pltpu.make_async_copy(b.at[r, :], o.at[r, :], out_s.at[n, k]))
    for cp in loads:
        cp.start()
    for cp, st in zip(loads, stores):
        cp.wait()
        st.start()
    for st in stores:
        st.wait()


def local(tokens, cotangent, routes, gates, w_gate, w_up, w_down):
    vmem = pl.BlockSpec(memory_space=pltpu.VMEM)
    any_spec = pl.BlockSpec(memory_space=pl.ANY)
    dma = pltpu.SemaphoreType.DMA
    out = pl.pallas_call(
        kernel,
        out_shape=(
            jax.ShapeDtypeStruct((TB, D), BF),
            jax.ShapeDtypeStruct((TB, D), BF),
            jax.ShapeDtypeStruct((D, H), BF),
            jax.ShapeDtypeStruct((D, H), BF),
            jax.ShapeDtypeStruct((H, D), BF),
        ),
        in_specs=[vmem] * 2 + [any_spec] * 5,
        out_specs=[any_spec] * 5,
        scratch_shapes=[
            pltpu.VMEM((4, 2, 2 * TOP, TB), F32),
            pltpu.VMEM((4, 2, 2 * TB, HD), BF),
            pltpu.VMEM((16, 2, 2, PAIR, HD), BF),
            pltpu.VMEM((2, ROWS, D), BF),
            pltpu.VMEM((3, ROWS, H), BF),
            pltpu.VMEM((2, 3, ROWS, Q // 2), BF),
            pltpu.VMEM((2, 3, ROWS, Q), BF),
            pltpu.VMEM((3, ROWS, H), BF),
            pltpu.VMEM((2, ROWS, D), BF),
            pltpu.VMEM((2, E * PAIR, HD), BF),
            pltpu.VMEM((2, E * PAIR, 2 * TB), BF),
            pltpu.VMEM((2, 2 * TB, HD), BF),
            pltpu.VMEM((3, 2, 2 * TB, HD), BF),
            pltpu.VMEM((D, H), BF),
            pltpu.VMEM((D, H), BF),
            pltpu.VMEM((H, D), BF),
            dma((4,)), dma((4,)), dma((6,)), dma((3,)), dma((4, 3)), dma((4, 3)),
            dma((16, 2)), dma((16, 2)), dma((NCH, 8)), dma((NCH, 8)),
            dma((16, 2)), dma((16, 2)), dma((4,)), dma((4,)), dma((2,)), dma((2,)), dma((2,)), dma((3,)),
        ],
        compiler_params=pltpu.CompilerParams(
            collective_id=0, has_side_effects=True, vmem_limit_bytes=62 * 1024 * 1024
        ),
    )(routes.T, gates.T, tokens, cotangent, w_gate.reshape(D, H), w_up.reshape(D, H), w_down.reshape(H, D))
    mixed, ingrad, gg, gu, gd = pl.pallas_call(
        settle,
        out_shape=[jax.ShapeDtypeStruct(o.shape, o.dtype) for o in out],
        in_specs=[pl.BlockSpec(memory_space=pltpu.HBM)] * 5,
        out_specs=[any_spec] * 5,
        scratch_shapes=[pltpu.VMEM((TB, D), BF), pltpu.VMEM((TB, D), BF), pltpu.VMEM((D, H), BF), pltpu.VMEM((D, H), BF), pltpu.VMEM((H, D), BF), dma((5, 4)), dma((5, 4))],
        compiler_params=pltpu.CompilerParams(vmem_limit_bytes=60 * 1024 * 1024),
    )(*out)
    return mixed, ingrad, gg[None], gu[None], gd[None]


def solution(mesh):
    in_specs = (
        P("expert", "dp"),
        P("expert", "dp"),
        P("expert", None),
        P("expert", None),
        P("expert", "dp", None),
        P("expert", "dp", None),
        P("expert", None, "dp"),
    )
    out_specs = (
        P("expert", "dp"),
        P("expert", "dp"),
        P("expert", "dp", None),
        P("expert", "dp", None),
        P("expert", None, "dp"),
    )
    return jax.shard_map(local, mesh=mesh, in_specs=in_specs, out_specs=out_specs, check_vma=False)
```

```python
import functools

import jax
import jax.numpy as jnp
from jax import lax
from jax.experimental import pallas as pl
from jax.experimental.pallas import tpu as pltpu
from jax.sharding import PartitionSpec as P

MESH = pl.DeviceIdType.MESH
BF = jnp.bfloat16
F32 = jnp.float32

TB = 128
TOP = 4
E = 32
CAP = 24
PAIR = 2 * CAP
D = 1792
HD = D // 2
H = 1024
ROWS = 768
Q = H // 4
SLOTS = (
    (1, 1), (1, 3), (3, 1), (1, 2), (2, 1), (0, 2), (2, 0),
    (2, 2), (3, 3), (2, 3), (3, 2), (0, 1), (1, 0), (0, 3), (3, 0), (0, 0),
)
SIZES = (3, 4, 4, 4, 1)
FIRST = tuple(sum(SIZES[:n]) for n in range(len(SIZES)))
NCH = len(SIZES)
NN = (((1,), (0,)), ((), ()))
NT = (((1,), (1,)), ((), ()))
TN = (((0,), (0,)), ((), ()))


def mm(a, b, dims):
    return lax.dot_general(a, b, dims, preferred_element_type=F32)


def kernel(
    routes, gates, tok, cot, wg, wu, wd,
    mixed, ingrad, ogg, ogu, ogd,
    p1, tokp, xd_send, xd_rows, part, r1, r2, act, or_send, or_recv, pt, res, cmb, vg, vu, vd,
    pair_s, pair_r, loc, wsem, ag_s, ag_r, ds_s, ds_r, x_s, x_r, cb_s, cb_r, gv_s, gv_r, fin_s, fin_r, fin_l, gsem,
):
    q = lax.axis_index("dp")
    e = lax.axis_index("expert")
    chip = e // 2
    core = e % 2
    other = 1 - core
    cz, cy = chip // 4, chip % 4
    right, left, opp = (q + 1) % 4, (q + 3) % 4, (q + 2) % 4
    partner = chip * 2 + other

    flip = core == 1
    pa, pb = jnp.where(flip, cy, cz), jnp.where(flip, cz, cy)

    def chip_at(a, b):
        a, b = a % 4, b % 4
        return jnp.where(flip, b * 4 + a, a * 4 + b)

    def slot(a, b):
        return jnp.where(flip, SLOTS.index((b, a)), SLOTS.index((a, b)))

    def half(c):
        return pl.ds(pl.multiple_of(c * HD, 128), HD)

    def rows48(j):
        return pl.ds(pl.multiple_of(j * PAIR, 16), PAIR)

    def blk(c):
        return pl.ds(pl.multiple_of(c * TB, TB), TB)

    local = [
        pltpu.make_async_copy(tok.at[:, half(core)], tokp.at[0, 0, blk(core), :], loc.at[2]),
        pltpu.make_async_copy(cot.at[:, half(core)], tokp.at[0, 1, blk(core), :], loc.at[3]),
    ]
    for cp in local:
        cp.start()

    bar = pltpu.get_barrier_semaphore()

    def greet(d, carry):
        @pl.when(d != e)
        def _():
            pl.semaphore_signal(bar, inc=1, device_id={"dp": q, "expert": d}, device_id_type=MESH)

        return carry

    for n in (right, left, opp):
        pl.semaphore_signal(bar, inc=1, device_id={"dp": n, "expert": e}, device_id_type=MESH)
    lax.fori_loop(0, E, greet, 0)
    pl.semaphore_wait(bar, 34)

    def remote(src, dst, ss, rs, dp, ex):
        return pltpu.make_async_remote_copy(
            src_ref=src, dst_ref=dst, send_sem=ss, recv_sem=rs,
            device_id={"dp": dp, "expert": ex}, device_id_type=MESH,
        )

    def pair_copies(c):
        return [
            remote(tok.at[:, half(1 - c)], tokp.at[0, 0, blk(c), :], pair_s.at[2], pair_r.at[2], q, partner),
            remote(cot.at[:, half(1 - c)], tokp.at[0, 1, blk(c), :], pair_s.at[3], pair_r.at[3], q, partner),
        ]

    def pair_rows(c):
        return remote(p1.at[0, c], p1.at[0, c], pair_s.at[0], pair_r.at[0], q, partner)

    mine = pair_copies(core)
    for cp in mine:
        cp.start()

    ids = lax.broadcasted_iota(jnp.int32, (E, TB), 0)
    picks = [routes[k : k + 1, :] == ids for k in range(TOP)]
    named = functools.reduce(jnp.logical_or, picks)
    earlier = lax.broadcasted_iota(jnp.int32, (TB, TB), 0) < lax.broadcasted_iota(jnp.int32, (TB, TB), 1)
    before = mm(jnp.where(named, 1.0, 0.0).astype(BF), jnp.where(earlier, 1.0, 0.0).astype(BF), NN)
    first = (core * CAP).astype(F32)
    for k in range(TOP):
        rank = jnp.sum(jnp.where(picks[k], before, 0.0), axis=0, keepdims=True)
        p1[0, core, k : k + 1, :] = routes[k : k + 1, :].astype(F32) * PAIR + rank + first
        p1[0, core, TOP + k : TOP + k + 1, :] = gates[k : k + 1, :]
    pair_rows(core).start()
    weights = [
        pltpu.make_async_copy(wg, vg, wsem.at[0]),
        pltpu.make_async_copy(wu, vu, wsem.at[1]),
        pltpu.make_async_copy(wd, vd, wsem.at[2]),
    ]
    for cp in weights:
        cp.start()
    for cp in local:
        cp.wait()
    for cp in pair_copies(other) + [pair_rows(other)]:
        cp.wait_recv()

    def spread(a):
        if a == 2:
            up, down = chip_at(pa + 1, pb) * 2 + core, chip_at(pa + 3, pb) * 2 + core
            return [
                remote(p1.at[1], p1.at[2], ag_s.at[2, 0], ag_r.at[2, 0], q, up),
                remote(tokp.at[1, 0], tokp.at[2, 0], ag_s.at[2, 1], ag_r.at[2, 1], q, up),
                remote(tokp.at[3, 1], tokp.at[2, 1], ag_s.at[2, 2], ag_r.at[2, 2], q, down),
            ]
        d = chip_at(pa + a, pb) * 2 + core
        return [
            remote(p1.at[0], p1.at[a], ag_s.at[a, 0], ag_r.at[a, 0], q, d),
            remote(tokp.at[0], tokp.at[a], ag_s.at[a, 1], ag_r.at[a, 1], q, d),
        ]

    def step_s(a):
        for cp in spread(a):
            cp.start()

    for a in (1, 3):
        step_s(a)

    def group(a, b):
        return pl.ds((4 * a + b) * 2 * PAIR, 2 * PAIR)

    def fill(a, b):
        d = chip_at(pa, pb + b)
        rid = (lax.broadcasted_iota(jnp.int32, (2 * PAIR, 2 * TB), 0) + d * (2 * PAIR)).astype(F32)
        one = jnp.zeros((2 * PAIR, 2 * TB), F32)
        gat = jnp.zeros((2 * PAIR, 2 * TB), F32)

        def of(row):
            return jnp.concatenate([p1[a, 0, row : row + 1, :], p1[a, 1, row : row + 1, :]], axis=1)

        for k in range(TOP):
            hit = rid == of(k)
            one = jnp.where(hit, 1.0, one)
            gat = jnp.where(hit, of(TOP + k), gat)
        one, gat = one.astype(BF), gat.astype(BF)
        pt[0, group(a, b)] = gat
        pt[1, group(a, b)] = one
        xs = mm(one, tokp[a, 0], NN).astype(BF)
        dsv = mm(gat, tokp[a, 1], NN).astype(BF)
        xd_send[4 * a + b, :, 0] = xs.reshape(2, PAIR, HD)
        xd_send[4 * a + b, :, 1] = dsv.reshape(2, PAIR, HD)

    def disp(a, b, k):
        c_dst = core if k == 0 else other
        j = slot(a, b)
        src, dst = xd_send.at[4 * a + b, c_dst], xd_rows.at[:, rows48(j), half(core)]
        if b == 0 and k == 0:
            return pltpu.make_async_copy(src, dst, ds_r.at[j, 0])
        return remote(src, dst, ds_s.at[j, k], ds_r.at[j, k], q, chip_at(pa, pb + b) * 2 + c_dst)

    def from_other(a, b):
        j = slot(a, b)
        return remote(
            xd_send.at[4 * a + b, core], xd_rows.at[:, rows48(j), half(other)],
            ds_s.at[j, 1], ds_r.at[j, 1], q, partner,
        )

    have = {0}

    def step_f(c):
        for a, b in sorted(SLOTS[FIRST[c] : FIRST[c] + SIZES[c]], key=lambda ab: (0, 1, 3, 2)[ab[0]]):
            if a not in have:
                have.add(a)
                for cp in spread(a):
                    cp.wait_recv()
            fill(a, b)
            disp(a, b, 0).start()
            disp(a, b, 1).start()

    def step_w(a):
        for cp in weights:
            cp.wait()

    def cols256(n):
        return pl.ds(pl.multiple_of(n * 256, 256), 256)

    def chunk(a):
        return pl.ds(FIRST[a] * PAIR, SIZES[a] * PAIR)

    def step_a(a):
        for sa, sb in SLOTS[FIRST[a] : FIRST[a] + SIZES[a]]:
            mine_in = disp(sa, sb, 0)
            if sb == 0:
                mine_in.wait()
            else:
                mine_in.wait_recv()
            from_other(sa, sb).wait_recv()

        def body(i, carry):
            cs = cols256((q + 2 + i) % 4)
            x = xd_rows[0, chunk(a), :]
            part[0, chunk(a), cs] = mm(x, vg[:, cs], NN).astype(BF)
            part[1, chunk(a), cs] = mm(x, vu[:, cs], NN).astype(BF)
            part[2, chunk(a), cs] = mm(xd_rows[1, chunk(a), :], vd[cs, :], NT).astype(BF)
            return carry

        body(0, 0)
        for cp in rs1(a):
            cp.start()
        lax.fori_loop(1, 4, body, 0)

    def cols(n):
        return pl.ds(pl.multiple_of(n * Q, Q), Q)

    def lower(n):
        return pl.ds(pl.multiple_of(n * Q, 128), Q // 2)

    def upper(n):
        return pl.ds(pl.multiple_of(n * Q + Q // 2, 128), Q // 2)

    def rs1(a):
        return [
            remote(part.at[:, chunk(a), lower(opp)], r1.at[0, :, chunk(a), :], x_s.at[a, 0], x_r.at[a, 0], right, e),
            remote(part.at[:, chunk(a), upper(opp)], r1.at[1, :, chunk(a), :], x_s.at[a, 1], x_r.at[a, 1], left, e),
        ]

    def rs2(a):
        return [
            remote(part.at[:, chunk(a), cols(right)], r2.at[0, :, chunk(a), :], x_s.at[a, 2], x_r.at[a, 2], right, e),
            remote(part.at[:, chunk(a), cols(left)], r2.at[1, :, chunk(a), :], x_s.at[a, 3], x_r.at[a, 3], left, e),
        ]

    def ag1(a, n):
        own = act.at[:, chunk(a), cols(n)]
        return [
            remote(own, own, x_s.at[a, 4], x_r.at[a, 4], right, e),
            remote(own, own, x_s.at[a, 5], x_r.at[a, 5], left, e),
        ]

    def ag2(a, n0, n1):
        b0 = act.at[:, chunk(a), lower(n0)]
        b1 = act.at[:, chunk(a), upper(n1)]
        return [
            remote(b0, b0, x_s.at[a, 6], x_r.at[a, 6], right, e),
            remote(b1, b1, x_s.at[a, 7], x_r.at[a, 7], left, e),
        ]

    def step_b(a):
        for cp in rs1(a):
            cp.wait_recv()
        s2 = rs2(a)
        part[:, chunk(a), lower(right)] = (part[:, chunk(a), lower(right)].astype(F32) + r1[0, :, chunk(a), :].astype(F32)).astype(BF)
        s2[0].start()
        part[:, chunk(a), upper(left)] = (part[:, chunk(a), upper(left)].astype(F32) + r1[1, :, chunk(a), :].astype(F32)).astype(BF)
        s2[1].start()

    def step_c(a):
        for cp in rs2(a):
            cp.wait_recv()

        def total(k):
            return part[k, chunk(a), cols(q)].astype(F32) + r2[0, k, chunk(a), :].astype(F32) + r2[1, k, chunk(a), :].astype(F32)

        g, u, hg = total(0), total(1), total(2)
        sig = jax.nn.sigmoid(g)
        act[0, chunk(a), cols(q)] = (g * sig * u).astype(BF)
        act[1, chunk(a), cols(q)] = (hg * u * sig * (1.0 + g * (1.0 - sig))).astype(BF)
        act[2, chunk(a), cols(q)] = (hg * g * sig).astype(BF)
        for cp in ag1(a, q):
            cp.start()

    def step_d(a):
        ag1(a, left)[0].wait_recv()
        ag1(a, right)[1].wait_recv()
        for cp in ag2(a, left, right):
            cp.start()

    def comb(a, b, k):
        rows = rows48(slot(a, b))
        n = 4 * a + b if k == 0 else 4 * b + a
        dst = or_recv.at[:, pl.ds(pl.multiple_of(n * 2 * PAIR + core * PAIR, 16), PAIR), :]
        if k == 0:
            src = or_send.at[:, rows, half(core)]
            if b == 0:
                return pltpu.make_async_copy(src, dst, cb_r.at[n, 0])
            return remote(src, dst, cb_s.at[n, 0], cb_r.at[n, 0], q, chip_at(pa, pb + 4 - b) * 2 + core)
        src = or_send.at[:, rows, half(other)]
        return remote(src, dst, cb_s.at[n, 1], cb_r.at[n, 1], q, chip_at(pa + 4 - a, pb) * 2 + other)

    def comb_other(a, b):
        n = 4 * a + b
        dst = or_recv.at[:, pl.ds(pl.multiple_of(n * 2 * PAIR + other * PAIR, 16), PAIR), :]
        return remote(or_send.at[:, rows48(0), half(core)], dst, cb_s.at[n, 1], cb_r.at[n, 1], q, partner)

    def give_far():
        down, up = chip_at(pa + 3, pb) * 2 + core, chip_at(pa + 1, pb) * 2 + core
        return [
            remote(tokp.at[2, 0], cmb.at[1, 0], gv_s.at[0], gv_r.at[0], q, down),
            remote(tokp.at[2, 1], cmb.at[1, 1], gv_s.at[2], gv_r.at[2], q, up),
        ]

    def give(a):
        return remote(tokp.at[a], cmb.at[a - 1], gv_s.at[a], gv_r.at[a], q, chip_at(pa + 4 - a, pb) * 2 + core)

    def added(a, k):
        r = pl.ds(a * 8 * PAIR, 8 * PAIR)
        return mm(pt[k, r, :], or_recv[k, r, :], TN)

    def step_g(a):
        if a == 2:
            for cp in spread(2):
                cp.wait_send()
        for b in range(4):
            cp = comb(a, b, 0)
            if b == 0:
                cp.wait()
            else:
                cp.wait_recv()
            comb_other(a, b).wait_recv()
        if a == 0:
            return
        passing = {1: 0, 3: 1}.get(a)
        for k in range(2):
            sums = added(a, k)
            if k == passing:
                give_far()[k].wait_recv()
                sums = sums + cmb[1, k].astype(F32)
            tokp[a, k] = sums.astype(BF)
        for cp in give_far() if a == 2 else [give(a)]:
            cp.start()

    def step_e(a):
        for cp in ag2(a, opp, opp):
            cp.wait_recv()

        def body(n, carry):
            cs = cols256(n)
            or_send[0, chunk(a), cs] = mm(act[0, chunk(a), :], vd[:, cs], NN).astype(BF)
            or_send[1, chunk(a), cs] = (
                mm(act[1, chunk(a), :], vg[cs, :], NT) + mm(act[2, chunk(a), :], vu[cs, :], NT)
            ).astype(BF)
            return carry

        lax.fori_loop(0, D // 256, body, 0)
        for sa, sb in SLOTS[FIRST[a] : FIRST[a] + SIZES[a]]:
            comb(sa, sb, 0).start()
            comb(sa, sb, 1).start()

    for step, a in (
        (step_f, 0), (step_s, 2), (step_f, 1), (step_f, 2), (step_w, 0), (step_a, 0), (step_f, 3), (step_b, 0), (step_f, 4), (step_a, 1), (step_c, 0), (step_b, 1), (step_d, 0), (step_a, 2), (step_c, 1), (step_e, 0), (step_b, 2), (step_d, 1), (step_a, 3), (step_c, 2), (step_e, 1), (step_b, 3), (step_d, 2), (step_a, 4), (step_c, 3), (step_e, 2), (step_b, 4), (step_d, 3), (step_c, 4), (step_e, 3), (step_g, 2), (step_d, 4), (step_g, 1), (step_g, 3), (step_e, 4),
    ):
        step(a)

    def grad_x(n, carry):
        cs = cols256(n)
        x = xd_rows[0, :, cs]
        vg[cs, :] = mm(x, act[1], TN).astype(BF)
        vu[cs, :] = mm(x, act[2], TN).astype(BF)
        return carry

    lax.fori_loop(0, D // 256, grad_x, 0)
    out_w = [
        pltpu.make_async_copy(vg, ogg, gsem.at[0]),
        pltpu.make_async_copy(vu, ogu, gsem.at[1]),
        pltpu.make_async_copy(vd, ogd, gsem.at[2]),
    ]
    out_w[0].start()
    out_w[1].start()

    def grad_d(n, carry):
        cs = cols256(n)
        vd[cs, :] = mm(act[0, :, cs], xd_rows[1], TN).astype(BF)
        return carry

    lax.fori_loop(0, H // 256, grad_d, 0)
    out_w[2].start()

    step_g(0)
    for a in (1, 3):
        give(a).wait_recv()
    fin = []
    for k, out in enumerate((mixed, ingrad)):
        far = cmb[0, k].astype(F32) + cmb[2, k].astype(F32)
        res[k] = (added(0, k) + far).astype(BF)
        away = remote(res.at[k, blk(other), :], out.at[:, half(core)], fin_s.at[k], fin_r.at[k], q, partner)
        here = pltpu.make_async_copy(res.at[k, blk(core), :], out.at[:, half(core)], fin_l.at[k])
        away.start()
        here.start()
        fin.append((away, here))

    for cp in mine + [pair_rows(core)]:
        cp.wait_send()
    for a in (1, 3):
        for cp in spread(a):
            cp.wait_send()
    for a, b in SLOTS:
        if b != 0:
            disp(a, b, 0).wait_send()
        disp(a, b, 1).wait_send()
    for a, b in SLOTS:
        if b != 0:
            comb(a, b, 0).wait_send()
        comb(a, b, 1).wait_send()
    for cp in [give(1), give(3)] + give_far():
        cp.wait_send()
    for a in range(NCH):
        for cp in rs1(a) + rs2(a) + ag1(a, q) + ag2(a, left, right):
            cp.wait_send()
    for cp in out_w:
        cp.wait()
    for k, out in enumerate((mixed, ingrad)):
        fin[k][0].wait_send()
        fin[k][1].wait()
        remote(res.at[k, blk(core), :], out.at[:, half(other)], fin_s.at[k], fin_r.at[k], q, partner).wait_recv()


def settle(i0, i1, i2, i3, i4, o0, o1, o2, o3, o4, b0, b1, b2, b3, b4, in_s, out_s):
    loads, stores = [], []
    for n, (i, b, o) in enumerate(zip((i2, i3, i4, i0, i1), (b2, b3, b4, b0, b1), (o2, o3, o4, o0, o1))):
        step = i.shape[0] // 4
        for k in range(4):
            r = pl.ds(k * step, step)
            loads.append(pltpu.make_async_copy(i.at[r, :], b.at[r, :], in_s.at[n, k]))
            stores.append(pltpu.make_async_copy(b.at[r, :], o.at[r, :], out_s.at[n, k]))
    for cp in loads:
        cp.start()
    for cp, st in zip(loads, stores):
        cp.wait()
        st.start()
    for st in stores:
        st.wait()


def local(tokens, cotangent, routes, gates, w_gate, w_up, w_down):
    vmem = pl.BlockSpec(memory_space=pltpu.VMEM)
    any_spec = pl.BlockSpec(memory_space=pl.ANY)
    dma = pltpu.SemaphoreType.DMA
    out = pl.pallas_call(
        kernel,
        out_shape=(
            jax.ShapeDtypeStruct((TB, D), BF),
            jax.ShapeDtypeStruct((TB, D), BF),
            jax.ShapeDtypeStruct((D, H), BF),
            jax.ShapeDtypeStruct((D, H), BF),
            jax.ShapeDtypeStruct((H, D), BF),
        ),
        in_specs=[vmem] * 2 + [any_spec] * 5,
        out_specs=[any_spec] * 5,
        scratch_shapes=[
            pltpu.VMEM((4, 2, 2 * TOP, TB), F32),
            pltpu.VMEM((4, 2, 2 * TB, HD), BF),
            pltpu.VMEM((16, 2, 2, PAIR, HD), BF),
            pltpu.VMEM((2, ROWS, D), BF),
            pltpu.VMEM((3, ROWS, H), BF),
            pltpu.VMEM((2, 3, ROWS, Q // 2), BF),
            pltpu.VMEM((2, 3, ROWS, Q), BF),
            pltpu.VMEM((3, ROWS, H), BF),
            pltpu.VMEM((2, ROWS, D), BF),
            pltpu.VMEM((2, E * PAIR, HD), BF),
            pltpu.VMEM((2, E * PAIR, 2 * TB), BF),
            pltpu.VMEM((2, 2 * TB, HD), BF),
            pltpu.VMEM((3, 2, 2 * TB, HD), BF),
            pltpu.VMEM((D, H), BF),
            pltpu.VMEM((D, H), BF),
            pltpu.VMEM((H, D), BF),
            dma((4,)), dma((4,)), dma((6,)), dma((3,)), dma((4, 3)), dma((4, 3)),
            dma((16, 2)), dma((16, 2)), dma((NCH, 8)), dma((NCH, 8)),
            dma((16, 2)), dma((16, 2)), dma((4,)), dma((4,)), dma((2,)), dma((2,)), dma((2,)), dma((3,)),
        ],
        compiler_params=pltpu.CompilerParams(
            collective_id=0, has_side_effects=True, vmem_limit_bytes=62 * 1024 * 1024
        ),
    )(routes.T, gates.T, tokens, cotangent, w_gate.reshape(D, H), w_up.reshape(D, H), w_down.reshape(H, D))
    mixed, ingrad, gg, gu, gd = pl.pallas_call(
        settle,
        out_shape=[jax.ShapeDtypeStruct(o.shape, o.dtype) for o in out],
        in_specs=[pl.BlockSpec(memory_space=pltpu.HBM)] * 5,
        out_specs=[any_spec] * 5,
        scratch_shapes=[pltpu.VMEM((TB, D), BF), pltpu.VMEM((TB, D), BF), pltpu.VMEM((D, H), BF), pltpu.VMEM((D, H), BF), pltpu.VMEM((H, D), BF), dma((5, 4)), dma((5, 4))],
        compiler_params=pltpu.CompilerParams(vmem_limit_bytes=60 * 1024 * 1024),
    )(*out)
    return mixed, ingrad, gg[None], gu[None], gd[None]


def solution(mesh):
    in_specs = (
        P("expert", "dp"),
        P("expert", "dp"),
        P("expert", None),
        P("expert", None),
        P("expert", "dp", None),
        P("expert", "dp", None),
        P("expert", None, "dp"),
    )
    out_specs = (
        P("expert", "dp"),
        P("expert", "dp"),
        P("expert", "dp", None),
        P("expert", "dp", None),
        P("expert", None, "dp"),
    )
    return jax.shard_map(local, mesh=mesh, in_specs=in_specs, out_specs=out_specs, check_vma=False)
```
